128 devices in a mesh: row: 16 (over z, y_hi, core), col: 8 (over y_lo, x).
Axes of the slice: x: 4, y: 4 (y_hi: 2, y_lo: 2; y = y_hi * 2 + y_lo), z: 4, core: 2. Of those that a mesh axis runs over, the one named last changes fastest.
Arguments:
- demand: float32 [4096, 8192], P('row', 'col'), may hold values from 0.2 to 2
- leakage: float32 [4096, 8192], P('row', 'col'), may hold values from 0.05 to 0.5
- conductance: float32 [4096, 8192], P('row', 'col'), may hold values from 0.5 to 4
- vias: int32 [4096, 8192], P('row', 'col'), may hold values 0 or 1
- layer_of: int32 [512, 1024], P('row'), may hold values from 0 to 63
- lateral_k: float32 [64, 512, 1024], P('col', 'row'), may hold values from 0.3 to 3
- vertical_k: float32 [64, 512, 1024], P('col', 'row'), may hold values from 0.1 to 1
Outputs:
- drop: float32 [4096, 8192], P('row', 'col')
- temperature: float32 [64, 512, 1024], P('col', 'row')
The draws below stay inside these ranges and needn't reach their ends.
All inputs are finite; a program needn't handle non-finite values. No bound on the sum of `vias` on one device may be relied on, other than what follows from the above.
Results may differ from the reference program's by a relative error of at most 0.0001.
Values sent between devices are 32-bit elements; how exact they have to be, the bound alone decides.
A program may use at most 128 MiB of HBM per device.

```python
import math
import jax
import jax.numpy as jnp

COARSE = 8
SWEEPS = 4
HEAT_SWEEPS = 4
OUTER = 2
POWER_ROWS = 4096
POWER_COLS = 8192
THERM_ROWS = 512
THERM_COLS = 1024
LAYERS = 64


def set_ends(result, own_key, smallest, top_value):
    extent = result.shape
    spot = [jax.random.randint(jax.random.fold_in(own_key, axis), (), 0, extent[axis]) for axis in range(len(extent))]
    result = result.at[tuple(spot)].set(smallest)
    longest = extent.index(max(extent))
    spot[longest] = (spot[longest] + 1) % extent[longest]
    return result.at[tuple(spot)].set(top_value)


def level_of(stream_key, dims, pieces, low, top_value):
    factor_of = 1.0
    for position, shards_of in pieces:
        steps = jax.random.uniform(jax.random.fold_in(jax.random.fold_in(stream_key, 6), position), (shards_of,), jnp.float32, low / len(pieces), top_value / len(pieces))
        factor_of = factor_of * jnp.repeat(jnp.exp(steps), dims[position] // shards_of).reshape((-1,) + (1,) * (len(dims) - 1 - position))
    return factor_of


def setup_inputs(seed: int = 0) -> dict:
    splits = jax.random.split(jax.random.key(seed), 8)
    return {
        "demand": jnp.clip(jnp.exp(math.log(2.0) - 2.3025851 * jax.random.uniform(splits[0], (POWER_ROWS, POWER_COLS), jnp.float32) ** level_of(splits[0], (POWER_ROWS, POWER_COLS), ((0, 16), (1, 8)), -0.2, 0.2)), 0.2, 2.0),
        "leakage": jnp.clip(jnp.exp(math.log(0.5) - 2.3025851 * jax.random.uniform(splits[1], (POWER_ROWS, POWER_COLS), jnp.float32) ** level_of(splits[1], (POWER_ROWS, POWER_COLS), ((0, 16), (1, 8)), -0.2, 0.2)), 0.05, 0.5),
        "conductance": jnp.clip(jnp.exp(math.log(4.0) - 2.0794415 * jax.random.uniform(splits[2], (POWER_ROWS, POWER_COLS), jnp.float32) ** level_of(splits[2], (POWER_ROWS, POWER_COLS), ((0, 16), (1, 8)), -0.2, 0.2)), 0.5, 4.0),
        "vias": set_ends((jax.random.randint(splits[3], (POWER_ROWS, POWER_COLS), 0, 8) < 1).astype(jnp.int32), jax.random.fold_in(splits[3], 1), 0, 1),
        "layer_of": set_ends(jax.random.randint(splits[4], (THERM_ROWS, THERM_COLS), 0, LAYERS), jax.random.fold_in(splits[4], 1), 0, LAYERS - 1).astype(jnp.int32),
        "lateral_k": jnp.clip(jnp.exp(math.log(3.0) - 2.3025851 * jax.random.uniform(splits[5], (LAYERS, THERM_ROWS, THERM_COLS), jnp.float32) ** level_of(splits[5], (LAYERS, THERM_ROWS, THERM_COLS), ((0, 8), (1, 16)), -0.2, 0.2)), 0.3, 3.0),
        "vertical_k": jnp.clip(jnp.exp(math.log(1.0) - 2.3025851 * jax.random.uniform(splits[6], (LAYERS, THERM_ROWS, THERM_COLS), jnp.float32) ** level_of(splits[6], (LAYERS, THERM_ROWS, THERM_COLS), ((0, 8), (1, 16)), -0.2, 0.2)), 0.1, 1.0),
    }


COND_SLOPE = 0.5
LEAK_SLOPE = 0.7
VIA_CONDUCT = 4.0


def fine_of(coarse):
    count_rows, count_cols = coarse.shape
    spread = jnp.broadcast_to(coarse[:, None, :, None], (count_rows, COARSE, count_cols, COARSE))
    return spread.reshape(count_rows * COARSE, count_cols * COARSE)


def coarse_of(fine):
    count_rows = fine.shape[0] // COARSE
    count_cols = fine.shape[1] // COARSE
    return jnp.mean(fine.reshape(count_rows, COARSE, count_cols, COARSE), axis=(1, 3))


def relax_power(drop, cond, load, via_g):
    drop_pad = jnp.pad(drop, 1)
    cond_pad = jnp.pad(cond, 1)
    w_north = (cond + cond_pad[:-2, 1:-1]) * 0.5
    w_south = (cond + cond_pad[2:, 1:-1]) * 0.5
    w_west = (cond + cond_pad[1:-1, :-2]) * 0.5
    w_east = (cond + cond_pad[1:-1, 2:]) * 0.5
    summed = load + w_north * drop_pad[:-2, 1:-1] + w_south * drop_pad[2:, 1:-1] + w_west * drop_pad[1:-1, :-2] + w_east * drop_pad[1:-1, 2:]
    return summed / (w_north + w_south + w_west + w_east + via_g)


def relax_thermal(temp, source, lateral_k, vertical_k):
    temp_pad = jnp.pad(temp, 1)
    lat_pad = jnp.pad(lateral_k, 1)
    vert_pad = jnp.pad(vertical_k, 1)
    w_north = (lateral_k + lat_pad[1:-1, :-2, 1:-1]) * 0.5
    w_south = (lateral_k + lat_pad[1:-1, 2:, 1:-1]) * 0.5
    w_west = (lateral_k + lat_pad[1:-1, 1:-1, :-2]) * 0.5
    w_east = (lateral_k + lat_pad[1:-1, 1:-1, 2:]) * 0.5
    w_below = (vertical_k + vert_pad[:-2, 1:-1, 1:-1]) * 0.5
    w_above = (vertical_k + vert_pad[2:, 1:-1, 1:-1]) * 0.5
    summed = source + w_north * temp_pad[1:-1, :-2, 1:-1] + w_south * temp_pad[1:-1, 2:, 1:-1] + w_west * temp_pad[1:-1, 1:-1, :-2] + w_east * temp_pad[1:-1, 1:-1, 2:] + w_below * temp_pad[:-2, 1:-1, 1:-1] + w_above * temp_pad[2:, 1:-1, 1:-1]
    return summed / (w_north + w_south + w_west + w_east + w_below + w_above)


def reference(demand, leakage, conductance, vias, layer_of, lateral_k, vertical_k):
    drop = jnp.zeros(demand.shape, jnp.float32)
    temp = jnp.zeros(lateral_k.shape, jnp.float32)
    via_g = VIA_CONDUCT * vias.astype(jnp.float32)
    layers = jnp.arange(lateral_k.shape[0], dtype=jnp.int32)
    picker = layer_of[None, :, :] == layers[:, None, None]
    cell_temp = jnp.zeros(layer_of.shape, jnp.float32)
    for outer in range(OUTER):
        if outer > 0:
            cell_temp = jnp.sum(jnp.where(picker, temp, jnp.zeros_like(temp)), axis=0)
        fine_temp = fine_of(cell_temp)
        cond = conductance / (1.0 + COND_SLOPE * fine_temp)
        load = demand + leakage * jnp.exp(LEAK_SLOPE * fine_temp)
        for sweep in range(SWEEPS):
            drop = relax_power(drop, cond, load, via_g)
        heat = coarse_of(load * (1.0 - drop) + cond * drop * drop)
        source = jnp.where(picker, heat[None, :, :], jnp.zeros_like(temp))
        for sweep in range(HEAT_SWEEPS):
            temp = relax_thermal(temp, source, lateral_k, vertical_k)
    return drop, temp
```

```python
import functools

import jax
import jax.numpy as jnp
from jax import lax
from jax.experimental import pallas as pl
from jax.experimental.pallas import tpu as pltpu
from jax.sharding import PartitionSpec as P

COARSE = 8
SWEEPS = 4
HEAT_SWEEPS = 4
COND_SLOPE = 0.5
LEAK_SLOPE = 0.7
VIA_CONDUCT = 4.0

MESH = pl.DeviceIdType.MESH
HIGH = lax.Precision.HIGHEST
F32 = jnp.float32
LINKS = 128


def reciprocal(value):
    return 1.0 / value


def pooled(left, right):
    return jnp.dot(left, right, precision=HIGH, preferred_element_type=F32)


def kernel(
    sizes,
    demand,
    leakage,
    conductance,
    vias,
    layer_of,
    lateral,
    vertical,
    drop_out,
    temp_out,
    p_cond,
    p_dem,
    p_leak,
    p_via,
    c_now,
    load,
    a_n,
    a_s,
    a_w,
    a_e,
    b_p,
    d_0,
    d_1,
    stage,
    stage_i,
    pl_send,
    pr_send,
    pl_recv,
    pr_recv,
    layers,
    lat,
    ver,
    t_n,
    t_s,
    t_w,
    t_e,
    t_b,
    t_a,
    t_r,
    b_t,
    r_far,
    temp_0,
    temp_1,
    pool,
    spread,
    rows_sum,
    heat_own,
    heat_all,
    part,
    part_recv,
    cell,
    g_up,
    e_up,
    load_sem,
    out_sem,
    send_sem,
    recv_sem,
):
    NR, NC, TR, GL, CR = sizes
    NT = 8
    TQ = TR // 4
    row = lax.axis_index("row")
    col = lax.axis_index("col")
    up, down = lax.rem(row + NR - 1, NR), lax.rem(row + 1, NR)
    left, right = lax.rem(col + NC - 1, NC), lax.rem(col + 1, NC)
    peers = [lax.rem(col + k, NC) for k in range(1, NC)]
    count = [0]

    def send(src, dst, device):
        slot = count[0]
        count[0] += 1
        copy = pltpu.make_async_remote_copy(
            src_ref=src,
            dst_ref=dst,
            send_sem=send_sem.at[slot],
            recv_sem=recv_sem.at[slot],
            device_id=device,
            device_id_type=MESH,
        )
        copy.start()
        return copy

    lane = lax.broadcasted_iota(jnp.int32, (8, 128), 1)
    sub = lax.broadcasted_iota(jnp.int32, (8, 128), 0)
    first_lane = lane == 0
    last_lane = lane == 127

    def west_east(tiles):
        n = len(tiles)
        plus = [pltpu.roll(x, 1, axis=1) for x in tiles]
        minus = [pltpu.roll(x, 127, axis=1) for x in tiles]
        west = [jnp.where(first_lane, plus[t - 1], plus[t]) for t in range(n)]
        east = [jnp.where(last_lane, minus[(t + 1) % n], minus[t]) for t in range(n)]
        return west, east

    power = ((conductance, p_cond), (demand, p_dem), (leakage, p_leak), (vias, p_via))
    for index, (src, dst) in enumerate(power):
        for t in range(NT):
            pltpu.make_async_copy(
                src.at[:, pl.ds(128 * t, 128)], dst.at[t, pl.ds(16, TR), :], load_sem.at[index]
            ).start()
    for t in range(NC):
        cut = pl.ds(128 * t, 128)
        pltpu.make_async_copy(
            lateral.at[:, :, cut], lat.at[:, t, pl.ds(8, CR), :], load_sem.at[4]
        ).start()
        pltpu.make_async_copy(
            vertical.at[:, :, cut], ver.at[pl.ds(1, GL), t], load_sem.at[5]
        ).start()
        pltpu.make_async_copy(layer_of.at[:, cut], layers.at[t], load_sem.at[6]).start()

    def loaded(index, ref):
        pltpu.make_async_copy(ref, ref, load_sem.at[index]).wait()

    barrier = pltpu.get_barrier_semaphore()
    near = [(row, p) for p in peers]
    near += [(r, c) for r in (up, down) for c in (col, left, right)]
    for device in near:
        pl.semaphore_signal(barrier, inc=1, device_id=device, device_id_type=MESH)
    pl.semaphore_wait(barrier, len(near))

    row_copies = []
    for index, src in enumerate((conductance, demand, leakage, vias)):
        for side, start, device in ((0, TR - 8, (down, col)), (1, 0, (up, col))):
            dst = stage_i.at[side] if index == 3 else stage.at[side, index]
            row_copies.append(send(src.at[pl.ds(start, 8), :], dst, device))
    ver_copies = []

    def pool_body(i, carry):
        r = lax.broadcasted_iota(jnp.int32, (128, 128), 0)
        c = lax.broadcasted_iota(jnp.int32, (128, 128), 1)
        start = pl.multiple_of(i * 128, 128)
        pool[pl.ds(start, 128), :] = jnp.where(16 * i + r // 8 == c, 1.0 / 64.0, 0.0)
        spread[i] = jnp.where(16 * i + c // 8 == r, 1.0, 0.0)
        return carry

    lax.fori_loop(0, NT, pool_body, 0)

    for index, (_, dst) in enumerate(power):
        loaded(index, dst.at[pl.ds(0, NT), pl.ds(16, TR), :])

    def pack_body(i, carry):
        base = pl.multiple_of(8 * i, 8)
        acc_l = acc_r = jnp.zeros((8, 128), F32)
        for q in range(4):
            for a, ref in enumerate((p_cond, p_dem, p_leak, p_via)):
                at = 32 * q + 8 * a
                rows = pl.ds(16 + q * TQ + base, 8)
                lo = ref[0, rows, :].astype(F32)
                hi = ref[NT - 1, rows, :].astype(F32)
                here = lane // 8 == at // 8
                acc_l = jnp.where(here, pltpu.roll(lo, at, axis=1), acc_l)
                acc_r = jnp.where(here, pltpu.roll(hi, (at + 8) % 128, axis=1), acc_r)
        pl_send[pl.ds(base, 8), :] = acc_l
        pr_send[pl.ds(base, 8), :] = acc_r
        return carry

    lax.fori_loop(0, TQ // 8, pack_body, 0)
    col_copies = []
    for src, dst, c in ((pl_send, pl_recv, left), (pr_send, pr_recv, right)):
        col_copies.append(send(src, dst.at[pl.ds(8, TQ), :], (row, c)))
        col_copies.append(send(src.at[pl.ds(TQ - 8, 8), :], dst.at[pl.ds(0, 8), :], (down, c)))
        col_copies.append(send(src.at[pl.ds(0, 8), :], dst.at[pl.ds(TQ + 8, 8), :], (up, c)))

    for t in range(NC):
        cut = pl.ds(128 * t, 128)
        ver_copies.append(send(vertical.at[GL - 1, :, cut], ver.at[0, t], (row, right)))
        ver_copies.append(send(vertical.at[0, :, cut], ver.at[GL + 1, t], (row, left)))

    def send_rows(ref, first):
        span = pl.ds(first, GL)
        return [
            send(
                ref.at[span, :, pl.ds(8, 1), :], ref.at[span, :, pl.ds(8 + CR, 1), :], (up, col)
            ),
            send(
                ref.at[span, :, pl.ds(7 + CR, 1), :], ref.at[span, :, pl.ds(7, 1), :], (down, col)
            ),
        ]

    loaded(4, lat.at[:, :, pl.ds(8, CR), :])
    lat_copies = send_rows(lat, 0)

    for copy in row_copies + col_copies:
        copy.wait_recv()
    has_up = jnp.where(row > 0, 1.0, 0.0).astype(F32)
    has_down = jnp.where(row < NR - 1, 1.0, 0.0).astype(F32)
    side_ok = jnp.logical_or(
        jnp.logical_and(lane < 64, col < NC - 1), jnp.logical_and(lane >= 64, col > 0)
    )
    for index, ref in enumerate((p_cond, p_dem, p_leak)):
        for t in range(NT):
            cut = slice(128 * t, 128 * t + 128)
            top = stage[0, index, :, cut]
            bottom = stage[1, index, :, cut]
            if index == 0:
                top, bottom = top * has_up, bottom * has_down
            ref[t, 8:16, :] = top
            ref[t, 16 + TR : 24 + TR, :] = bottom
    for t in range(NT):
        cut = slice(128 * t, 128 * t + 128)
        p_via[t, 8:16, :] = stage_i[0, :, cut]
        p_via[t, 16 + TR : 24 + TR, :] = stage_i[1, :, cut]

    def rim(a, q, from_right, from_left):
        at = 32 * q + 8 * a
        value = jnp.where(
            lane < 64,
            pltpu.roll(from_right, (128 - at) % 128, axis=1),
            pltpu.roll(from_left, (248 - at) % 128, axis=1),
        )
        if a == 0:
            return jnp.where(side_ok, value, 0.0)
        if a == 3:
            return value.astype(jnp.int32)
        return value

    def unpack_body(i, carry):
        base = pl.multiple_of(8 * i, 8)
        from_right = pl_recv[pl.ds(8 + base, 8), :]
        from_left = pr_recv[pl.ds(8 + base, 8), :]
        for a, ref in enumerate((p_cond, p_dem, p_leak, p_via)):
            for q in range(4):
                ref[NT, pl.ds(16 + q * TQ + base, 8), :] = rim(a, q, from_right, from_left)
        return carry

    lax.fori_loop(0, TQ // 8, unpack_body, 0)
    for a, ref in enumerate((p_cond, p_dem, p_leak, p_via)):
        top = rim(a, 3, pl_recv[0:8, :], pr_recv[0:8, :])
        bottom = rim(a, 0, pl_recv[TQ + 8 : TQ + 16, :], pr_recv[TQ + 8 : TQ + 16, :])
        if a == 0:
            top, bottom = top * has_up, bottom * has_down
        ref[NT, 8:16, :] = top
        ref[NT, 16 + TR : 24 + TR, :] = bottom

    last_tile = TR // 8 + 1

    def power_coefs(c_ref, with_load):
        def coef_body(i, carry):
            base = pl.multiple_of(8 + 8 * i, 8)
            row_ok = jnp.logical_and(
                jnp.logical_or(i > 0, row > 0), jnp.logical_or(i < last_tile, row < NR - 1)
            )
            rows = pl.ds(base, 8)
            centers = [c_ref[t, rows, :] for t in range(NT + 1)]
            west, east = west_east(centers)
            for t in range(NT + 1):
                c = centers[t]
                c_n = c + c_ref[t, pl.ds(base - 1, 8), :]
                c_s = c + c_ref[t, pl.ds(base + 1, 8), :]
                c_w = c + west[t]
                c_e = c + east[t]
                denom = 0.5 * ((c_n + c_s) + (c_w + c_e)) + VIA_CONDUCT * p_via[
                    t, rows, :
                ].astype(F32)
                ok = row_ok if t < NT else jnp.logical_and(side_ok, row_ok)
                inverse = jnp.where(ok, reciprocal(denom), 0.0)
                half = 0.5 * inverse
                a_n[t, rows, :] = c_n * half
                a_s[t, rows, :] = c_s * half
                a_w[t, rows, :] = c_w * half
                a_e[t, rows, :] = c_e * half
                if with_load:
                    value = p_dem[t, rows, :] + p_leak[t, rows, :]
                    load[t, rows, :] = value
                else:
                    value = load[t, rows, :]
                b_p[t, rows, :] = value * inverse
            return carry

        lax.fori_loop(0, TR // 8 + 2, coef_body, 0)

    def power_sweep(src, dst):
        def sweep_body(j, carry):
            for i in range(2):
                base = pl.multiple_of(8 + 16 * j + 8 * i, 8)
                rows = pl.ds(base, 8)
                west, east = west_east([src[t, rows, :] for t in range(NT + 1)])
                for t in range(NT + 1):
                    dst[t, rows, :] = (
                        b_p[t, rows, :]
                        + a_n[t, rows, :] * src[t, pl.ds(base - 1, 8), :]
                        + a_s[t, rows, :] * src[t, pl.ds(base + 1, 8), :]
                    ) + (a_w[t, rows, :] * west[t] + a_e[t, rows, :] * east[t])
            return carry

        lax.fori_loop(0, TR // 16 + 1, sweep_body, 0)

    def send_heat(c_ref, d_ref, work, phase):
        def heat_body(i, carry):
            rows = pl.ds(pl.multiple_of(16 + 8 * i, 8), 8)
            for t in range(NT):
                d = d_ref[t, rows, :]
                work[t, rows, :] = load[t, rows, :] * (1.0 - d) + c_ref[t, rows, :] * d * d
            return carry

        lax.fori_loop(0, TR // 8, heat_body, 0)
        for j in range(CR // 8):
            for t in range(NT):
                total = work[t, pl.ds(16 + 64 * j, 8, stride=8), :]
                for k in range(1, 8):
                    total = total + work[t, pl.ds(16 + 64 * j + k, 8, stride=8), :]
                rows_sum[8 * j : 8 * j + 8, 128 * t : 128 * t + 128] = total
        heat = pooled(rows_sum[...], pool[...])
        heat_own[phase] = heat
        heat_all[phase, col] = heat
        return [
            send(heat_own.at[phase], heat_all.at[phase, col], (row, peer)) for peer in peers
        ]

    def thermal_coefs(layer):
        low = jnp.logical_and(layer == 0, col == 0)
        high = jnp.logical_and(layer == GL - 1, col == NC - 1)
        for i in range(CR // 8):
            rows = pl.ds(8 * i, 8)
            centers = [lat[layer, t, pl.ds(8 + 8 * i, 8), :] for t in range(NC)]
            west, east = west_east(centers)
            for t in range(NC):
                k, k_w, k_e = centers[t], west[t], east[t]
                k_n = lat[layer, t, pl.ds(7 + 8 * i, 8), :]
                k_s = lat[layer, t, pl.ds(9 + 8 * i, 8), :]
                v = ver[layer + 1, t, rows, :]
                v_b = jnp.where(low, 0.0, ver[layer, t, rows, :])
                v_a = jnp.where(high, 0.0, ver[layer + 2, t, rows, :])
                edge_n = edge_s = edge_w = edge_e = None
                if i == 0:
                    edge_n = jnp.logical_and(sub == 0, row == 0)
                    k_n = jnp.where(edge_n, 0.0, k_n)
                if i == CR // 8 - 1:
                    edge_s = jnp.logical_and(sub == 7, row == NR - 1)
                    k_s = jnp.where(edge_s, 0.0, k_s)
                if t == 0:
                    edge_w = first_lane
                    k_w = jnp.where(edge_w, 0.0, k_w)
                if t == NC - 1:
                    edge_e = last_lane
                    k_e = jnp.where(edge_e, 0.0, k_e)
                sums = [k + k_n, k + k_s, k + k_w, k + k_e, v + v_b, v + v_a]
                twice = ((sums[0] + sums[1]) + (sums[2] + sums[3])) + (sums[4] + sums[5])
                inverse = reciprocal(twice)
                t_r[layer, t, rows, :] = 2.0 * inverse
                edges = (edge_n, edge_s, edge_w, edge_e, low, high)
                for ref, total, edge in zip((t_n, t_s, t_w, t_e, t_b, t_a), sums, edges):
                    value = total * inverse
                    if edge is not None:
                        value = jnp.where(edge, 0.0, value)
                    ref[layer, t, rows, :] = value

    def sources(phase, start):
        def source_body(layer, carry):
            for i in range(CR // 8):
                rows = pl.ds(8 * i, 8)
                for t in range(NC):
                    here = layers[t, rows, :] == col * GL + layer
                    value = (
                        jnp.where(here, heat_all[phase, t, rows, :], 0.0) * t_r[layer, t, rows, :]
                    )
                    b_t[layer, t, rows, :] = value
                    if start:
                        temp_0[layer + 1, t, pl.ds(8 + 8 * i, 8), :] = value
            return carry

        lax.fori_loop(0, GL, source_body, 0)
        if start:
            for side, target, layer in ((0, 0, -1), (1, GL + 1, GL)):
                for i in range(CR // 8):
                    rows = pl.ds(8 * i, 8)
                    for t in range(NC):
                        here = layers[t, rows, :] == col * GL + layer
                        temp_0[target, t, pl.ds(8 + 8 * i, 8), :] = (
                            jnp.where(here, heat_all[phase, t, rows, :], 0.0)
                            * r_far[side, t, rows, :]
                        )

    def thermal_layer(src, dst, layer):
        for i in range(CR // 8):
            rows = pl.ds(8 * i, 8)
            mid = pl.ds(8 + 8 * i, 8)
            west, east = west_east([src[layer + 1, t, mid, :] for t in range(NC)])
            for t in range(NC):
                dst[layer + 1, t, mid, :] = (
                    (
                        b_t[layer, t, rows, :]
                        + t_n[layer, t, rows, :] * src[layer + 1, t, pl.ds(7 + 8 * i, 8), :]
                    )
                    + (
                        t_s[layer, t, rows, :] * src[layer + 1, t, pl.ds(9 + 8 * i, 8), :]
                        + t_b[layer, t, rows, :] * src[layer, t, mid, :]
                    )
                    + (
                        t_a[layer, t, rows, :] * src[layer + 2, t, mid, :]
                        + t_w[layer, t, rows, :] * west[t]
                    )
                ) + t_e[layer, t, rows, :] * east[t]

    def send_planes(ref):
        mid = pl.ds(8, CR)
        return [
            send(ref.at[GL, :, mid, :], ref.at[0, :, mid, :], (row, right)),
            send(ref.at[1, :, mid, :], ref.at[GL + 1, :, mid, :], (row, left)),
        ]

    def faces(body):
        def face_body(j, carry):
            body(j * (GL - 1))
            return carry

        lax.fori_loop(0, 2, face_body, 0)

    def interior(body):
        def interior_body(j, carry):
            body(j)
            return carry

        lax.fori_loop(1, GL - 1, interior_body, 0)

    power_coefs(p_cond, True)
    loaded(5, ver.at[pl.ds(1, GL)])
    loaded(6, layers)
    for copy in ver_copies + lat_copies:
        copy.wait_recv()
    faces(thermal_coefs)
    r_copies = [
        send(t_r.at[GL - 1], r_far.at[0], (row, right)),
        send(t_r.at[0], r_far.at[1], (row, left)),
    ]
    power_sweep(b_p, d_0)
    power_sweep(d_0, d_1)
    power_sweep(d_1, d_0)
    heat_copies = send_heat(p_cond, d_0, d_1, 0)
    interior(thermal_coefs)
    for copy in heat_copies + r_copies:
        copy.wait_recv()
    sources(0, True)
    pending = list(row_copies + col_copies + ver_copies + lat_copies + r_copies + heat_copies)

    levels = {1: send_rows(temp_0, 1)}
    in_flight = {1: levels[1]}

    def sweep(level, planes_now, rows_now):
        src, dst = (temp_0, temp_1) if level % 2 == 0 else (temp_1, temp_0)
        for copy in in_flight[level - 1]:
            copy.wait_recv()
        for copy in in_flight.pop(level - 2, []):
            copy.wait_send()
        faces(functools.partial(thermal_layer, src, dst))
        started = send_planes(dst) if planes_now else []
        interior(functools.partial(thermal_layer, src, dst))
        if rows_now:
            started += send_rows(dst, 1)
        in_flight[level] = started

    sweep(2, True, True)
    sweep(3, True, True)
    sweep(4, False, False)

    def part_body(i, carry):
        base = pl.multiple_of(8 * i, 8)
        for t in range(NC):
            ids = layers[t, pl.ds(base, 8), :] - col * GL
            total = jnp.zeros((8, 128), F32)
            for layer in range(GL):
                total = jnp.where(
                    ids == layer, temp_1[layer + 1, t, pl.ds(8 + base, 8), :], total
                )
            part[t, pl.ds(base, 8), :] = total
        return carry

    lax.fori_loop(0, CR // 8, part_body, 0)
    part_copies = [
        send(part.at[peer], part_recv.at[k], (row, peer)) for k, peer in enumerate(peers)
    ]
    in_flight[4] = send_planes(temp_1) + send_rows(temp_1, 1)
    for copy in part_copies:
        copy.wait_recv()
    total = part[col]
    for k in range(NC - 1):
        total = total + part_recv[k]
    cell[1, 8 : 8 + CR, :] = total
    own = cell.at[1, pl.ds(8, CR), :]
    low_rows = cell.at[1, pl.ds(8, 8), :]
    high_rows = cell.at[1, pl.ds(CR, 8), :]
    above, below = pl.ds(0, 8), pl.ds(8 + CR, 8)
    cell_copies = [
        send(own, cell.at[0, pl.ds(8, CR), :], (row, right)),
        send(own, cell.at[2, pl.ds(8, CR), :], (row, left)),
    ]
    for place, c in ((1, col), (0, right), (2, left)):
        cell_copies.append(send(high_rows, cell.at[place, above, :], (down, c)))
        cell_copies.append(send(low_rows, cell.at[place, below, :], (up, c)))
    for copy in cell_copies:
        copy.wait_recv()
    for target, shape in (
        (g_up, lambda x: reciprocal(1.0 + COND_SLOPE * x)),
        (e_up, lambda x: jnp.exp(LEAK_SLOPE * x)),
    ):
        coarse = shape(cell[1])
        for t in range(NT):
            target[t] = pooled(coarse, spread[t])
        from_left = jnp.broadcast_to(shape(cell[0])[:, 127:128], (CR + 16, 128))
        from_right = jnp.broadcast_to(shape(cell[2])[:, 0:1], (CR + 16, 128))
        wide = lax.broadcasted_iota(jnp.int32, (CR + 16, 128), 1)
        target[NT] = jnp.where(wide < 64, from_right, from_left)

    def warm_body(i, carry):
        rows = pl.ds(pl.multiple_of(8 + 8 * i, 8), 8)
        coarse = pl.ds(7 + i, 1)
        for t in range(NT + 1):
            c_now[t, rows, :] = p_cond[t, rows, :] * g_up[t, coarse, :]
            load[t, rows, :] = p_dem[t, rows, :] + p_leak[t, rows, :] * e_up[t, coarse, :]
        return carry

    lax.fori_loop(0, TR // 8 + 2, warm_body, 0)
    power_coefs(c_now, False)
    power_sweep(d_0, d_1)
    power_sweep(d_1, d_0)
    power_sweep(d_0, d_1)
    power_sweep(d_1, d_0)
    heat_copies = send_heat(c_now, d_0, d_1, 1)
    for t in range(NT):
        pltpu.make_async_copy(
            d_0.at[t, pl.ds(16, TR), :], drop_out.at[:, pl.ds(128 * t, 128)], out_sem.at[0]
        ).start()
    for copy in heat_copies:
        copy.wait_recv()
    sources(1, False)
    pending += part_copies + cell_copies + heat_copies
    sweep(5, True, True)
    sweep(6, True, True)
    sweep(7, True, True)
    sweep(8, False, False)
    for t in range(NC):
        pltpu.make_async_copy(
            temp_1.at[pl.ds(1, GL), t, pl.ds(8, CR), :],
            temp_out.at[:, :, pl.ds(128 * t, 128)],
            out_sem.at[1],
        ).start()
    for copies in in_flight.values():
        pending += copies
    for copy in pending:
        copy.wait_send()
    done = d_0.at[pl.ds(0, NT), pl.ds(16, TR), :]
    pltpu.make_async_copy(done, done, out_sem.at[0]).wait()
    done = temp_1.at[pl.ds(1, GL), :, pl.ds(8, CR), :]
    pltpu.make_async_copy(done, done, out_sem.at[1]).wait()


def body(num_rows, num_cols, demand, leakage, conductance, vias, layer_of, lateral_k, vertical_k):
    tile_rows, tile_cols = demand.shape
    group_layers, cell_rows, therm_cols = lateral_k.shape
    sizes = (num_rows, num_cols, tile_rows, group_layers, cell_rows)
    fine = pltpu.VMEM((9, tile_rows + 32, 128), F32)
    slab = pltpu.VMEM((group_layers, num_cols, cell_rows, 128), F32)
    coarse = (cell_rows, 128)
    hbm = pl.BlockSpec(memory_space=pl.ANY)
    return pl.pallas_call(
        functools.partial(kernel, sizes),
        out_shape=(
            jax.ShapeDtypeStruct(demand.shape, F32),
            jax.ShapeDtypeStruct(lateral_k.shape, F32),
        ),
        in_specs=[hbm] * 7,
        out_specs=(hbm, hbm),
        scratch_shapes=[fine] * 3
        + [pltpu.VMEM((9, tile_rows + 32, 128), jnp.int32)]
        + [fine] * 9
        + [
            pltpu.VMEM((2, 3, 8, tile_cols), F32),
            pltpu.VMEM((2, 8, tile_cols), jnp.int32),
            pltpu.VMEM((tile_rows // 4, 128), F32),
            pltpu.VMEM((tile_rows // 4, 128), F32),
            pltpu.VMEM((tile_rows // 4 + 16, 128), F32),
            pltpu.VMEM((tile_rows // 4 + 16, 128), F32),
            pltpu.VMEM((num_cols,) + coarse, jnp.int32),
            pltpu.VMEM((group_layers, num_cols, cell_rows + 16, 128), F32),
            pltpu.VMEM((group_layers + 2, num_cols, cell_rows, 128), F32),
        ]
        + [slab] * 8
        + [
            pltpu.VMEM((2, num_cols) + coarse, F32),
            pltpu.VMEM((group_layers + 2, num_cols, cell_rows + 16, 128), F32),
            pltpu.VMEM((group_layers + 2, num_cols, cell_rows + 16, 128), F32),
            pltpu.VMEM((tile_cols, 128), F32),
            pltpu.VMEM((8, 128, 128), F32),
            pltpu.VMEM((cell_rows, tile_cols), F32),
            pltpu.VMEM((2,) + coarse, F32),
            pltpu.VMEM((2, num_cols) + coarse, F32),
            pltpu.VMEM((num_cols,) + coarse, F32),
            pltpu.VMEM((num_cols - 1,) + coarse, F32),
            pltpu.VMEM((3, cell_rows + 16, 128), F32),
            pltpu.VMEM((9, cell_rows + 16, 128), F32),
            pltpu.VMEM((9, cell_rows + 16, 128), F32),
            pltpu.SemaphoreType.DMA((7,)),
            pltpu.SemaphoreType.DMA((2,)),
            pltpu.SemaphoreType.DMA((LINKS,)),
            pltpu.SemaphoreType.DMA((LINKS,)),
        ],
        compiler_params=pltpu.CompilerParams(
            collective_id=0, has_side_effects=True, vmem_limit_bytes=52 << 20
        ),
        name="coupled",
    )(demand, leakage, conductance, vias, layer_of, lateral_k, vertical_k)


def solution(mesh):
    in_specs = (
        P("row", "col"),
        P("row", "col"),
        P("row", "col"),
        P("row", "col"),
        P("row", None),
        P("col", "row", None),
        P("col", "row", None),
    )
    out_specs = (P("row", "col"), P("col", "row", None))
    step = functools.partial(body, mesh.shape["row"], mesh.shape["col"])
    return jax.shard_map(step, mesh=mesh, in_specs=in_specs, out_specs=out_specs, check_vma=False)
```

```python
import functools

import jax
import jax.numpy as jnp
from jax import lax
from jax.experimental import pallas as pl
from jax.experimental.pallas import tpu as pltpu
from jax.sharding import PartitionSpec as P

COARSE = 8
SWEEPS = 4
HEAT_SWEEPS = 4
COND_SLOPE = 0.5
LEAK_SLOPE = 0.7
VIA_CONDUCT = 4.0

MESH = pl.DeviceIdType.MESH
F32 = jnp.float32
BF16 = jnp.bfloat16
LINKS = 128
COEF_TILES = 4
HALVES = 2


def reciprocal(value):
    return 1.0 / value


def pooled(left, right):
    parts = []
    for _ in range(3):
        part = left.astype(BF16).astype(F32)
        parts.append(part)
        left = left - part
    count = left.shape[0]
    stacked = jnp.concatenate(parts, axis=0).astype(BF16)
    product = jnp.dot(stacked, right, preferred_element_type=F32)
    return (product[2 * count :] + product[count : 2 * count]) + product[:count]


def kernel(
    sizes,
    demand,
    leakage,
    conductance,
    vias,
    layer_of,
    lateral,
    vertical,
    drop_out,
    temp_out,
    p_cond,
    p_dem,
    p_leak,
    p_via,
    c_now,
    load,
    a_n,
    a_s,
    a_w,
    a_e,
    b_p,
    d_0,
    d_1,
    stage,
    stage_i,
    pl_send,
    pr_send,
    pl_recv,
    pr_recv,
    layers,
    lat,
    ver,
    t_n,
    t_s,
    t_w,
    t_e,
    t_b,
    t_a,
    t_r,
    b_t,
    r_far,
    temp_0,
    temp_1,
    pool,
    spread,
    rows_sum,
    rim_send,
    rim_recv,
    heat_own,
    heat_all,
    part,
    part_recv,
    cell,
    g_up,
    e_up,
    load_sem,
    send_sem,
    recv_sem,
):
    NR, NC, TR, GL, CR = sizes
    NT = 8
    TQ = TR // 4
    row = lax.axis_index("row")
    col = lax.axis_index("col")
    up, down = lax.rem(row + NR - 1, NR), lax.rem(row + 1, NR)
    left, right = lax.rem(col + NC - 1, NC), lax.rem(col + 1, NC)
    peers = [lax.rem(col + k, NC) for k in range(1, NC)]
    count = [0]

    def send(src, dst, device):
        slot = count[0]
        count[0] += 1
        copy = pltpu.make_async_remote_copy(
            src_ref=src,
            dst_ref=dst,
            send_sem=send_sem.at[slot],
            recv_sem=recv_sem.at[slot],
            device_id=device,
            device_id_type=MESH,
        )
        copy.start()
        return copy

    lane = lax.broadcasted_iota(jnp.int32, (8, 128), 1)
    sub = lax.broadcasted_iota(jnp.int32, (8, 128), 0)
    first_lane = lane == 0
    last_lane = lane == 127

    def west_east(tiles):
        n = len(tiles)
        plus = [pltpu.roll(x, 1, axis=1) for x in tiles]
        minus = [pltpu.roll(x, 127, axis=1) for x in tiles]
        west = [jnp.where(first_lane, plus[t - 1], plus[t]) for t in range(n)]
        east = [jnp.where(last_lane, minus[(t + 1) % n], minus[t]) for t in range(n)]
        return west, east

    barrier = pltpu.get_barrier_semaphore()
    near = [(row, p) for p in peers]
    near += [(r, c) for r in (up, down) for c in (col, left, right)]
    for device in near:
        pl.semaphore_signal(barrier, inc=1, device_id=device, device_id_type=MESH)

    power = ((conductance, p_cond), (demand, p_dem), (leakage, p_leak), (vias, p_via))
    outer_tiles, inner_tiles = (0, NT - 1), tuple(range(1, NT - 1))
    for offset, tiles in ((0, outer_tiles), (7, inner_tiles)):
        for index, (src, dst) in enumerate(power):
            for t in tiles:
                pltpu.make_async_copy(
                    src.at[:, pl.ds(128 * t, 128)],
                    dst.at[t, pl.ds(16, TR), :],
                    load_sem.at[offset + index],
                ).start()
    for t in range(NC):
        cut = pl.ds(128 * t, 128)
        pltpu.make_async_copy(
            lateral.at[:, :, cut], lat.at[:, t, pl.ds(8, CR), :], load_sem.at[4]
        ).start()
        pltpu.make_async_copy(
            vertical.at[:, :, cut], ver.at[pl.ds(1, GL), t], load_sem.at[5]
        ).start()
        pltpu.make_async_copy(layer_of.at[:, cut], layers.at[t], load_sem.at[6]).start()

    def loaded(index, ref):
        pltpu.make_async_copy(ref, ref, load_sem.at[index]).wait()

    pl.semaphore_wait(barrier, len(near))

    row_copies = []
    for index, src in enumerate((conductance, demand, leakage, vias)):
        for side, start, device in ((0, TR - 8, (down, col)), (1, 0, (up, col))):
            dst = stage_i.at[side] if index == 3 else stage.at[side, index]
            row_copies.append(send(src.at[pl.ds(start, 8), :], dst, device))

    for index, (_, dst) in enumerate(power):
        loaded(index, dst.at[pl.ds(0, 2), pl.ds(16, TR), :])

    def pack_body(i, carry):
        base = pl.multiple_of(8 * i, 8)
        acc_l = acc_r = jnp.zeros((8, 128), F32)
        for q in range(4):
            for a, ref in enumerate((p_cond, p_dem, p_leak, p_via)):
                at = 32 * q + 8 * a
                rows = pl.ds(16 + q * TQ + base, 8)
                lo = ref[0, rows, :].astype(F32)
                hi = ref[NT - 1, rows, :].astype(F32)
                here = lane // 8 == at // 8
                acc_l = jnp.where(here, pltpu.roll(lo, at, axis=1), acc_l)
                acc_r = jnp.where(here, pltpu.roll(hi, (at + 8) % 128, axis=1), acc_r)
        pl_send[pl.ds(base, 8), :] = acc_l
        pr_send[pl.ds(base, 8), :] = acc_r
        return carry

    lax.fori_loop(0, TQ // 8, pack_body, 0)
    col_copies = []
    for src, dst, c in ((pl_send, pl_recv, left), (pr_send, pr_recv, right)):
        col_copies.append(send(src, dst.at[pl.ds(8, TQ), :], (row, c)))
        col_copies.append(send(src.at[pl.ds(TQ - 8, 8), :], dst.at[pl.ds(0, 8), :], (down, c)))
        col_copies.append(send(src.at[pl.ds(0, 8), :], dst.at[pl.ds(TQ + 8, 8), :], (up, c)))

    def send_rows(ref, first):
        span = pl.ds(first, GL)
        return [
            send(
                ref.at[span, :, pl.ds(8, 1), :], ref.at[span, :, pl.ds(8 + CR, 1), :], (up, col)
            ),
            send(
                ref.at[span, :, pl.ds(7 + CR, 1), :], ref.at[span, :, pl.ds(7, 1), :], (down, col)
            ),
        ]

    loaded(4, lat.at[:, :, pl.ds(8, CR), :])
    lat_copies = send_rows(lat, 0)
    ver_copies = []
    for t in range(NC):
        cut = pl.ds(128 * t, 128)
        ver_copies.append(send(vertical.at[GL - 1, :, cut], ver.at[0, t], (row, right)))
        ver_copies.append(send(vertical.at[0, :, cut], ver.at[GL + 1, t], (row, left)))

    def pool_body(i, carry):
        r = lax.broadcasted_iota(jnp.int32, (128, 128), 0)
        c = lax.broadcasted_iota(jnp.int32, (128, 128), 1)
        start = pl.multiple_of(i * 128, 128)
        pool[pl.ds(start, 128), :] = jnp.where(16 * i + r // 8 == c, 1.0 / 64.0, 0.0).astype(BF16)
        spread[i] = jnp.where(16 * i + c // 8 == r, 1.0, 0.0).astype(BF16)
        return carry

    lax.fori_loop(0, NT, pool_body, 0)
    for index, (_, dst) in enumerate(power):
        loaded(7 + index, dst.at[pl.ds(1, NT - 2), pl.ds(16, TR), :])

    for copy in row_copies + col_copies:
        copy.wait_recv()
    has_up = jnp.where(row > 0, 1.0, 0.0).astype(F32)
    has_down = jnp.where(row < NR - 1, 1.0, 0.0).astype(F32)
    side_ok = jnp.logical_or(
        jnp.logical_and(lane < 64, col < NC - 1), jnp.logical_and(lane >= 64, col > 0)
    )
    for index, ref in enumerate((p_cond, p_dem, p_leak)):
        for t in range(NT):
            cut = slice(128 * t, 128 * t + 128)
            top = stage[0, index, :, cut]
            bottom = stage[1, index, :, cut]
            if index == 0:
                top, bottom = top * has_up, bottom * has_down
            ref[t, 8:16, :] = top
            ref[t, 16 + TR : 24 + TR, :] = bottom
    for t in range(NT):
        cut = slice(128 * t, 128 * t + 128)
        p_via[t, 8:16, :] = stage_i[0, :, cut]
        p_via[t, 16 + TR : 24 + TR, :] = stage_i[1, :, cut]

    def rim(a, q, from_right, from_left):
        at = 32 * q + 8 * a
        value = jnp.where(
            lane < 64,
            pltpu.roll(from_right, (128 - at) % 128, axis=1),
            pltpu.roll(from_left, (248 - at) % 128, axis=1),
        )
        if a == 0:
            return jnp.where(side_ok, value, 0.0)
        if a == 3:
            return value.astype(jnp.int32)
        return value

    def unpack_body(i, carry):
        base = pl.multiple_of(8 * i, 8)
        from_right = pl_recv[pl.ds(8 + base, 8), :]
        from_left = pr_recv[pl.ds(8 + base, 8), :]
        for a, ref in enumerate((p_cond, p_dem, p_leak, p_via)):
            for q in range(4):
                ref[NT, pl.ds(16 + q * TQ + base, 8), :] = rim(a, q, from_right, from_left)
        return carry

    lax.fori_loop(0, TQ // 8, unpack_body, 0)
    for a, ref in enumerate((p_cond, p_dem, p_leak, p_via)):
        top = rim(a, 3, pl_recv[0:8, :], pr_recv[0:8, :])
        bottom = rim(a, 0, pl_recv[TQ + 8 : TQ + 16, :], pr_recv[TQ + 8 : TQ + 16, :])
        if a == 0:
            top, bottom = top * has_up, bottom * has_down
        ref[NT, 8:16, :] = top
        ref[NT, 16 + TR : 24 + TR, :] = bottom

    last_tile = TR // 8 + 1

    def power_coefs(c_ref, with_load):
        def coef_tile(i):
            base = pl.multiple_of(8 + 8 * i, 8)
            row_ok = jnp.logical_and(
                jnp.logical_or(i > 0, row > 0), jnp.logical_or(i < last_tile, row < NR - 1)
            )
            rows = pl.ds(base, 8)
            centers = [c_ref[t, rows, :] for t in range(NT + 1)]
            west, east = west_east(centers)
            for t in range(NT + 1):
                c = centers[t]
                c_n = c + c_ref[t, pl.ds(base - 1, 8), :]
                c_s = c + c_ref[t, pl.ds(base + 1, 8), :]
                c_w = c + west[t]
                c_e = c + east[t]
                denom = 0.5 * ((c_n + c_s) + (c_w + c_e)) + VIA_CONDUCT * p_via[
                    t, rows, :
                ].astype(F32)
                ok = row_ok if t < NT else jnp.logical_and(side_ok, row_ok)
                inverse = jnp.where(ok, reciprocal(denom), 0.0)
                half = 0.5 * inverse
                a_n[t, rows, :] = c_n * half
                a_s[t, rows, :] = c_s * half
                a_w[t, rows, :] = c_w * half
                a_e[t, rows, :] = c_e * half
                if with_load:
                    value = p_dem[t, rows, :] + p_leak[t, rows, :]
                    load[t, rows, :] = value
                else:
                    value = load[t, rows, :]
                b_p[t, rows, :] = value * inverse

        def coef_body(j, carry):
            for k in range(COEF_TILES):
                coef_tile(COEF_TILES * j + k)
            return carry

        lax.fori_loop(0, pl.cdiv(TR // 8 + 2, COEF_TILES), coef_body, 0)

    def power_sweep(src, dst):
        per = (TR // 8 + 2) // HALVES

        def sweep_body(j, carry):
            for i in range(per):
                base = pl.multiple_of(8 + 8 * (per * j + i), 8)
                rows = pl.ds(base, 8)
                west, east = west_east([src[t, rows, :] for t in range(NT + 1)])
                for t in range(NT + 1):
                    dst[t, rows, :] = (
                        b_p[t, rows, :]
                        + a_n[t, rows, :] * src[t, pl.ds(base - 1, 8), :]
                        + a_s[t, rows, :] * src[t, pl.ds(base + 1, 8), :]
                    ) + (a_w[t, rows, :] * west[t] + a_e[t, rows, :] * east[t])
            return carry

        lax.fori_loop(0, HALVES, sweep_body, 0)

    def send_heat(c_ref, d_ref, work, phase):
        def heat_body(i, carry):
            for k in range(4):
                rows = pl.ds(pl.multiple_of(16 + 32 * i + 8 * k, 8), 8)
                for t in range(NT):
                    d = d_ref[t, rows, :]
                    work[t, rows, :] = load[t, rows, :] * (1.0 - d) + c_ref[t, rows, :] * d * d
                    if phase == 1:
                        out_rows = pl.ds(pl.multiple_of(32 * i + 8 * k, 8), 8)
                        drop_out[out_rows, 128 * t : 128 * t + 128] = d
            return carry

        lax.fori_loop(0, TR // 32, heat_body, 0)
        for j in range(CR // 8):
            for t in range(NT):
                total = work[t, pl.ds(16 + 64 * j, 8, stride=8), :]
                for k in range(1, 8):
                    total = total + work[t, pl.ds(16 + 64 * j + k, 8, stride=8), :]
                rows_sum[8 * j : 8 * j + 8, 128 * t : 128 * t + 128] = total
        heat = pooled(rows_sum[...], pool[...])
        heat_own[phase] = heat
        heat_all[phase, col] = heat
        return [
            send(heat_own.at[phase], heat_all.at[phase, col], (row, peer)) for peer in peers
        ]

    def thermal_coefs(layer):
        low = jnp.logical_and(layer == 0, col == 0)
        high = jnp.logical_and(layer == GL - 1, col == NC - 1)
        for i in range(CR // 8):
            rows = pl.ds(8 * i, 8)
            centers = [lat[layer, t, pl.ds(8 + 8 * i, 8), :] for t in range(NC)]
            west, east = west_east(centers)
            for t in range(NC):
                k, k_w, k_e = centers[t], west[t], east[t]
                k_n = lat[layer, t, pl.ds(7 + 8 * i, 8), :]
                k_s = lat[layer, t, pl.ds(9 + 8 * i, 8), :]
                v = ver[layer + 1, t, rows, :]
                v_b = jnp.where(low, 0.0, ver[layer, t, rows, :])
                v_a = jnp.where(high, 0.0, ver[layer + 2, t, rows, :])
                edge_n = edge_s = edge_w = edge_e = None
                if i == 0:
                    edge_n = jnp.logical_and(sub == 0, row == 0)
                    k_n = jnp.where(edge_n, 0.0, k_n)
                if i == CR // 8 - 1:
                    edge_s = jnp.logical_and(sub == 7, row == NR - 1)
                    k_s = jnp.where(edge_s, 0.0, k_s)
                if t == 0:
                    edge_w = first_lane
                    k_w = jnp.where(edge_w, 0.0, k_w)
                if t == NC - 1:
                    edge_e = last_lane
                    k_e = jnp.where(edge_e, 0.0, k_e)
                sums = [k + k_n, k + k_s, k + k_w, k + k_e, v + v_b, v + v_a]
                twice = ((sums[0] + sums[1]) + (sums[2] + sums[3])) + (sums[4] + sums[5])
                inverse = reciprocal(twice)
                t_r[layer, t, rows, :] = 2.0 * inverse
                edges = (edge_n, edge_s, edge_w, edge_e, low, high)
                for ref, total, edge in zip((t_n, t_s, t_w, t_e, t_b, t_a), sums, edges):
                    value = total * inverse
                    if edge is not None:
                        value = jnp.where(edge, 0.0, value)
                    ref[layer, t, rows, :] = value

    def sources(phase, start):
        def source_body(layer, carry):
            for i in range(CR // 8):
                rows = pl.ds(8 * i, 8)
                for t in range(NC):
                    here = layers[t, rows, :] == col * GL + layer
                    value = (
                        jnp.where(here, heat_all[phase, t, rows, :], 0.0) * t_r[layer, t, rows, :]
                    )
                    b_t[layer, t, rows, :] = value
                    if start:
                        temp_0[layer + 1, t, pl.ds(8 + 8 * i, 8), :] = value
            return carry

        lax.fori_loop(0, GL, source_body, 0)
        if start:
            for side, target, layer in ((0, 0, -1), (1, GL + 1, GL)):
                for i in range(CR // 8):
                    rows = pl.ds(8 * i, 8)
                    for t in range(NC):
                        here = layers[t, rows, :] == col * GL + layer
                        temp_0[target, t, pl.ds(8 + 8 * i, 8), :] = (
                            jnp.where(here, heat_all[phase, t, rows, :], 0.0)
                            * r_far[side, t, rows, :]
                        )

    half = NC // 2
    chunks = (range(half), range(half, NC))
    tall = CR // 8
    edge_tiles = sorted({0, tall - 1})
    mid_tiles = [i for i in range(tall) if i not in edge_tiles]

    def thermal_block(src, dst, first, depth, row_tiles, tiles, out=None):
        cache = {}

        def at(k, i, t):
            if (k, i, t) not in cache:
                cache[k, i, t] = src[first + k, t, pl.ds(8 + 8 * i, 8), :]
            return cache[k, i, t]

        for k in range(depth):
            layer = first + k
            for i in row_tiles:
                rows = pl.ds(8 * i, 8)
                plus = {
                    t: pltpu.roll(at(k + 1, i, t), 1, axis=1)
                    for t in range(max(tiles[0] - 1, 0), tiles[-1] + 1)
                }
                minus = {
                    t: pltpu.roll(at(k + 1, i, t), 127, axis=1)
                    for t in range(tiles[0], min(tiles[-1] + 2, NC))
                }
                for t in tiles:
                    west = plus[t] if t == 0 else jnp.where(first_lane, plus[t - 1], plus[t])
                    east = minus[t] if t == NC - 1 else jnp.where(last_lane, minus[t + 1], minus[t])
                    value = (
                        (
                            b_t[layer, t, rows, :]
                            + t_n[layer, t, rows, :] * src[layer + 1, t, pl.ds(7 + 8 * i, 8), :]
                        )
                        + (
                            t_s[layer, t, rows, :] * src[layer + 1, t, pl.ds(9 + 8 * i, 8), :]
                            + t_b[layer, t, rows, :] * at(k, i, t)
                        )
                        + (t_a[layer, t, rows, :] * at(k + 2, i, t))
                        + (t_w[layer, t, rows, :] * west + t_e[layer, t, rows, :] * east)
                    )
                    if out is None:
                        dst[layer + 1, t, pl.ds(8 + 8 * i, 8), :] = value
                    else:
                        out[layer, rows, 128 * t : 128 * t + 128] = value

    def inner_layers(src, dst, row_tiles, out=None):
        depth = (GL - 2) // 2

        def inner_body(j, carry):
            thermal_block(src, dst, 1 + depth * j, depth, row_tiles, range(NC), out)
            return carry

        if row_tiles:
            lax.fori_loop(0, 2, inner_body, 0)

    def send_planes(ref, chunk):
        mid, tiles = pl.ds(8, CR), pl.ds(chunk[0], len(chunk))
        return [
            send(ref.at[GL, tiles, mid, :], ref.at[0, tiles, mid, :], (row, right)),
            send(ref.at[1, tiles, mid, :], ref.at[GL + 1, tiles, mid, :], (row, left)),
        ]

    def send_rims(ref, level):
        def rim_body(layer, carry):
            for t in range(NC):
                rim_send[level - 1, 0, t, pl.ds(layer, 1), :] = ref[layer + 1, t, pl.ds(8, 1), :]
                rim_send[level - 1, 1, t, pl.ds(layer, 1), :] = ref[
                    layer + 1, t, pl.ds(7 + CR, 1), :
                ]
            return carry

        lax.fori_loop(0, GL, rim_body, 0)
        return [
            send(rim_send.at[level - 1, side], rim_recv.at[level - 1, side], (r, col))
            for side, r in ((0, up), (1, down))
        ]

    def place_rims(ref, level):
        def place_body(layer, carry):
            for t in range(NC):
                ref[layer + 1, t, pl.ds(8 + CR, 1), :] = rim_recv[
                    level - 1, 0, t, pl.ds(layer, 1), :
                ]
                ref[layer + 1, t, pl.ds(7, 1), :] = rim_recv[level - 1, 1, t, pl.ds(layer, 1), :]
            return carry

        lax.fori_loop(0, GL, place_body, 0)

    def faces(body):
        def face_body(j, carry):
            body(j * (GL - 1))
            return carry

        lax.fori_loop(0, 2, face_body, 0)

    def interior(body):
        def interior_body(j, carry):
            body(j)
            return carry

        lax.fori_loop(1, GL - 1, interior_body, 0)

    power_coefs(p_cond, True)
    loaded(5, ver.at[pl.ds(1, GL)])
    loaded(6, layers)
    for copy in ver_copies + lat_copies:
        copy.wait_recv()
    faces(thermal_coefs)
    r_copies = [
        send(t_r.at[GL - 1], r_far.at[0], (row, right)),
        send(t_r.at[0], r_far.at[1], (row, left)),
    ]
    power_sweep(b_p, d_0)
    power_sweep(d_0, d_1)
    power_sweep(d_1, d_0)
    heat_copies = send_heat(p_cond, d_0, d_1, 0)
    interior(thermal_coefs)
    for copy in heat_copies + r_copies:
        copy.wait_recv()
    sources(0, True)
    pending = list(row_copies + col_copies + ver_copies + lat_copies + r_copies + heat_copies)

    rims = {1: send_rims(temp_0, 1)}
    planes = {}

    def sweep(level, exchange=True, out=None):
        src, dst = (temp_0, temp_1) if level % 2 == 0 else (temp_1, temp_0)
        for copies in planes.get(level - 2, ()):
            for copy in copies:
                copy.wait_send()
        for copy in rims[level - 1]:
            copy.wait_recv()
        place_rims(src, level - 1)
        sent = []
        for index, chunk in enumerate(chunks):
            if level - 1 in planes:
                for copy in planes[level - 1][index]:
                    copy.wait_recv()
            for layer in (0, GL - 1):
                thermal_block(src, dst, layer, 1, range(tall), chunk, out)
            if exchange:
                sent.append(send_planes(dst, chunk))
        if exchange:
            planes[level] = sent
            inner_layers(src, dst, edge_tiles)
            rims[level] = send_rims(dst, level)
            inner_layers(src, dst, mid_tiles)
        else:
            inner_layers(src, dst, list(range(tall)), out)

    sweep(2)
    sweep(3)
    sweep(4, False)

    def part_body(i, carry):
        base = pl.multiple_of(8 * i, 8)
        for t in range(NC):
            ids = layers[t, pl.ds(base, 8), :] - col * GL
            total = jnp.zeros((8, 128), F32)
            for layer in range(GL):
                total = jnp.where(
                    ids == layer, temp_1[layer + 1, t, pl.ds(8 + base, 8), :], total
                )
            part[t, pl.ds(base, 8), :] = total
        return carry

    lax.fori_loop(0, CR // 8, part_body, 0)
    part_copies = [
        send(part.at[peer], part_recv.at[k], (row, peer)) for k, peer in enumerate(peers)
    ]
    rims[4] = send_rims(temp_1, 4)
    planes[4] = [send_planes(temp_1, chunk) for chunk in chunks]
    for copy in part_copies:
        copy.wait_recv()
    total = part[col]
    for k in range(NC - 1):
        total = total + part_recv[k]
    cell[1, 8 : 8 + CR, :] = total
    own = cell.at[1, pl.ds(8, CR), :]
    low_rows = cell.at[1, pl.ds(8, 8), :]
    high_rows = cell.at[1, pl.ds(CR, 8), :]
    above, below = pl.ds(0, 8), pl.ds(8 + CR, 8)
    cell_copies = [
        send(own, cell.at[0, pl.ds(8, CR), :], (row, right)),
        send(own, cell.at[2, pl.ds(8, CR), :], (row, left)),
    ]
    for place, c in ((1, col), (0, right), (2, left)):
        cell_copies.append(send(high_rows, cell.at[place, above, :], (down, c)))
        cell_copies.append(send(low_rows, cell.at[place, below, :], (up, c)))
    shapes = (
        (g_up, lambda x: reciprocal(1.0 + COND_SLOPE * x)),
        (e_up, lambda x: jnp.exp(LEAK_SLOPE * x)),
    )
    for target, shape in shapes:
        coarse = shape(total)
        for t in range(NT):
            target[t, 8 : 8 + CR, :] = pooled(coarse, spread[t])

    def warm_tile(i, tiles):
        rows = pl.ds(pl.multiple_of(8 + 8 * i, 8), 8)
        coarse = pl.ds(7 + i, 1)
        for t in tiles:
            c_now[t, rows, :] = p_cond[t, rows, :] * g_up[t, coarse, :]
            load[t, rows, :] = p_dem[t, rows, :] + p_leak[t, rows, :] * e_up[t, coarse, :]

    def warm_body(j, carry):
        for k in range(4):
            warm_tile(1 + 4 * j + k, range(NT))
        return carry

    lax.fori_loop(0, TR // 32, warm_body, 0)
    for copy in cell_copies:
        copy.wait_recv()
    for target, shape in shapes:
        coarse = shape(jnp.concatenate([cell[1, 0:8, :], cell[1, 8 + CR : 16 + CR, :]], axis=0))
        for t in range(NT):
            rims_up = pooled(coarse, spread[t])
            target[t, 0:8, :] = rims_up[0:8]
            target[t, 8 + CR : 16 + CR, :] = rims_up[8:16]
        from_left = jnp.broadcast_to(shape(cell[0])[:, 127:128], (CR + 16, 128))
        from_right = jnp.broadcast_to(shape(cell[2])[:, 0:1], (CR + 16, 128))
        wide = lax.broadcasted_iota(jnp.int32, (CR + 16, 128), 1)
        target[NT] = jnp.where(wide < 64, from_right, from_left)
    warm_tile(0, range(NT))
    warm_tile(last_tile, range(NT))

    def warm_side_body(j, carry):
        for k in range(2):
            warm_tile(2 * j + k, (NT,))
        return carry

    lax.fori_loop(0, TR // 16 + 1, warm_side_body, 0)

    power_coefs(c_now, False)
    power_sweep(d_0, d_1)
    power_sweep(d_1, d_0)
    power_sweep(d_0, d_1)
    power_sweep(d_1, d_0)
    heat_copies = send_heat(c_now, d_0, d_1, 1)
    for copy in heat_copies:
        copy.wait_recv()
    sources(1, False)
    pending += part_copies + cell_copies + heat_copies
    sweep(5)
    sweep(6)
    sweep(7)
    sweep(8, False, temp_out)
    for copies in rims.values():
        pending += copies
    for copies in planes[7]:
        pending += copies
    for copy in pending:
        copy.wait_send()


def body(num_rows, num_cols, demand, leakage, conductance, vias, layer_of, lateral_k, vertical_k):
    tile_rows, tile_cols = demand.shape
    group_layers, cell_rows, therm_cols = lateral_k.shape
    sizes = (num_rows, num_cols, tile_rows, group_layers, cell_rows)
    fine = pltpu.VMEM((9, tile_rows + 48, 128), F32)
    slab = pltpu.VMEM((group_layers, num_cols, cell_rows, 128), F32)
    coarse = (cell_rows, 128)
    hbm = pl.BlockSpec(memory_space=pl.ANY)
    return pl.pallas_call(
        functools.partial(kernel, sizes),
        out_shape=(
            jax.ShapeDtypeStruct(demand.shape, F32),
            jax.ShapeDtypeStruct(lateral_k.shape, F32),
        ),
        in_specs=[hbm] * 7,
        out_specs=(pl.BlockSpec(memory_space=pltpu.VMEM),) * 2,
        scratch_shapes=[fine] * 3
        + [pltpu.VMEM((9, tile_rows + 48, 128), jnp.int32)]
        + [fine] * 9
        + [
            pltpu.VMEM((2, 3, 8, tile_cols), F32),
            pltpu.VMEM((2, 8, tile_cols), jnp.int32),
            pltpu.VMEM((tile_rows // 4, 128), F32),
            pltpu.VMEM((tile_rows // 4, 128), F32),
            pltpu.VMEM((tile_rows // 4 + 16, 128), F32),
            pltpu.VMEM((tile_rows // 4 + 16, 128), F32),
            pltpu.VMEM((num_cols,) + coarse, jnp.int32),
            pltpu.VMEM((group_layers, num_cols, cell_rows + 16, 128), F32),
            pltpu.VMEM((group_layers + 2, num_cols, cell_rows, 128), F32),
        ]
        + [slab] * 8
        + [
            pltpu.VMEM((2, num_cols) + coarse, F32),
            pltpu.VMEM((group_layers + 2, num_cols, cell_rows + 16, 128), F32),
            pltpu.VMEM((group_layers + 2, num_cols, cell_rows + 16, 128), F32),
            pltpu.VMEM((tile_cols, 128), BF16),
            pltpu.VMEM((8, 128, 128), BF16),
            pltpu.VMEM((cell_rows, tile_cols), F32),
            pltpu.VMEM((7, 2, num_cols, group_layers, 128), F32),
            pltpu.VMEM((7, 2, num_cols, group_layers, 128), F32),
            pltpu.VMEM((2,) + coarse, F32),
            pltpu.VMEM((2, num_cols) + coarse, F32),
            pltpu.VMEM((num_cols,) + coarse, F32),
            pltpu.VMEM((num_cols - 1,) + coarse, F32),
            pltpu.VMEM((3, cell_rows + 16, 128), F32),
            pltpu.VMEM((9, cell_rows + 16, 128), F32),
            pltpu.VMEM((9, cell_rows + 16, 128), F32),
            pltpu.SemaphoreType.DMA((11,)),
            pltpu.SemaphoreType.DMA((LINKS,)),
            pltpu.SemaphoreType.DMA((LINKS,)),
        ],
        compiler_params=pltpu.CompilerParams(
            collective_id=0, has_side_effects=True, vmem_limit_bytes=52 << 20
        ),
        name="coupled",
    )(demand, leakage, conductance, vias, layer_of, lateral_k, vertical_k)


def solution(mesh):
    in_specs = (
        P("row", "col"),
        P("row", "col"),
        P("row", "col"),
        P("row", "col"),
        P("row", None),
        P("col", "row", None),
        P("col", "row", None),
    )
    out_specs = (P("row", "col"), P("col", "row", None))
    step = functools.partial(body, mesh.shape["row"], mesh.shape["col"])
    return jax.shard_map(step, mesh=mesh, in_specs=in_specs, out_specs=out_specs, check_vma=False)
```

```python
import functools

import jax
import jax.numpy as jnp
from jax import lax
from jax.experimental import pallas as pl
from jax.experimental.pallas import tpu as pltpu
from jax.sharding import PartitionSpec as P

COARSE = 8
SWEEPS = 4
HEAT_SWEEPS = 4
COND_SLOPE = 0.5
LEAK_SLOPE = 0.7
VIA_CONDUCT = 4.0

MESH = pl.DeviceIdType.MESH
F32 = jnp.float32
BF16 = jnp.bfloat16
LINKS = 128
COEF_TILES = 4
HALVES = 2


def reciprocal(value):
    return 1.0 / value


def pooled(left, right):
    parts = []
    for _ in range(3):
        part = left.astype(BF16).astype(F32)
        parts.append(part)
        left = left - part
    count = left.shape[0]
    stacked = jnp.concatenate(parts, axis=0).astype(BF16)
    product = jnp.dot(stacked, right, preferred_element_type=F32)
    return (product[2 * count :] + product[count : 2 * count]) + product[:count]


def kernel(
    sizes,
    demand,
    leakage,
    conductance,
    vias,
    layer_of,
    lateral,
    vertical,
    drop_out,
    temp_out,
    p_cond,
    p_dem,
    p_leak,
    p_via,
    c_now,
    load,
    a_n,
    a_s,
    a_w,
    a_e,
    b_p,
    d_0,
    d_1,
    stage,
    stage_i,
    pl_send,
    pr_send,
    pl_recv,
    pr_recv,
    layers,
    lat,
    ver,
    t_n,
    t_s,
    t_w,
    t_e,
    t_b,
    t_a,
    t_r,
    b_t,
    temp_0,
    temp_1,
    pool,
    spread,
    rows_sum,
    heat_own,
    heat_all,
    part,
    part_recv,
    cell,
    g_up,
    e_up,
    load_sem,
    send_sem,
    recv_sem,
):
    NR, NC, TR, GL, CR = sizes
    NT = 8
    TQ = TR // 4
    row = lax.axis_index("row")
    col = lax.axis_index("col")
    up, down = lax.rem(row + NR - 1, NR), lax.rem(row + 1, NR)
    left, right = lax.rem(col + NC - 1, NC), lax.rem(col + 1, NC)
    peers = [lax.rem(col + k, NC) for k in range(1, NC)]
    count = [0]

    def send(src, dst, device):
        slot = count[0]
        count[0] += 1
        copy = pltpu.make_async_remote_copy(
            src_ref=src,
            dst_ref=dst,
            send_sem=send_sem.at[slot],
            recv_sem=recv_sem.at[slot],
            device_id=device,
            device_id_type=MESH,
        )
        copy.start()
        return copy

    lane = lax.broadcasted_iota(jnp.int32, (8, 128), 1)
    sub = lax.broadcasted_iota(jnp.int32, (8, 128), 0)
    first_lane = lane == 0
    last_lane = lane == 127

    def west_east(tiles):
        n = len(tiles)
        plus = [pltpu.roll(x, 1, axis=1) for x in tiles]
        minus = [pltpu.roll(x, 127, axis=1) for x in tiles]
        west = [jnp.where(first_lane, plus[t - 1], plus[t]) for t in range(n)]
        east = [jnp.where(last_lane, minus[(t + 1) % n], minus[t]) for t in range(n)]
        return west, east

    barrier = pltpu.get_barrier_semaphore()
    near = [(row, p) for p in peers]
    near += [(r, c) for r in (up, down) for c in (col, *peers)]
    for device in near:
        pl.semaphore_signal(barrier, inc=1, device_id=device, device_id_type=MESH)

    power = ((conductance, p_cond), (demand, p_dem), (leakage, p_leak), (vias, p_via))
    outer_tiles, inner_tiles = (0, NT - 1), tuple(range(1, NT - 1))
    for offset, tiles in ((0, outer_tiles), (7, inner_tiles)):
        for index, (src, dst) in enumerate(power):
            for t in tiles:
                pltpu.make_async_copy(
                    src.at[:, pl.ds(128 * t, 128)],
                    dst.at[t, pl.ds(16, TR), :],
                    load_sem.at[offset + index],
                ).start()
    for t in range(NC):
        cut = pl.ds(128 * t, 128)
        pltpu.make_async_copy(
            lateral.at[:, :, cut], lat.at[pl.ds(4, GL), t, pl.ds(12, CR), :], load_sem.at[4]
        ).start()
        pltpu.make_async_copy(
            vertical.at[:, :, cut], ver.at[pl.ds(4, GL), t, pl.ds(4, CR), :], load_sem.at[5]
        ).start()
        pltpu.make_async_copy(layer_of.at[:, cut], layers.at[t, pl.ds(8, CR), :], load_sem.at[6]).start()

    def loaded(index, ref):
        pltpu.make_async_copy(ref, ref, load_sem.at[index]).wait()

    for index, (_, dst) in enumerate(power):
        loaded(index, dst.at[pl.ds(0, 2), pl.ds(16, TR), :])

    def pack_body(i, carry):
        base = pl.multiple_of(8 * i, 8)
        acc_l = acc_r = jnp.zeros((8, 128), F32)
        for q in range(4):
            for a, ref in enumerate((p_cond, p_dem, p_leak, p_via)):
                at = 32 * q + 8 * a
                rows = pl.ds(16 + q * TQ + base, 8)
                lo = ref[0, rows, :].astype(F32)
                hi = ref[NT - 1, rows, :].astype(F32)
                here = lane // 8 == at // 8
                acc_l = jnp.where(here, pltpu.roll(lo, at, axis=1), acc_l)
                acc_r = jnp.where(here, pltpu.roll(hi, (at + 8) % 128, axis=1), acc_r)
        pl_send[pl.ds(base, 8), :] = acc_l
        pr_send[pl.ds(base, 8), :] = acc_r
        return carry

    lax.fori_loop(0, TQ // 8, pack_body, 0)
    pl.semaphore_wait(barrier, len(near))

    row_copies = []
    for index, src in enumerate((conductance, demand, leakage, vias)):
        for side, start, device in ((0, TR - 8, (down, col)), (1, 0, (up, col))):
            dst = stage_i.at[side] if index == 3 else stage.at[side, index]
            row_copies.append(send(src.at[pl.ds(start, 8), :], dst, device))

    col_copies = []
    for src, dst, c in ((pl_send, pl_recv, left), (pr_send, pr_recv, right)):
        col_copies.append(send(src, dst.at[pl.ds(8, TQ), :], (row, c)))
        col_copies.append(send(src.at[pl.ds(TQ - 8, 8), :], dst.at[pl.ds(0, 8), :], (down, c)))
        col_copies.append(send(src.at[pl.ds(0, 8), :], dst.at[pl.ds(TQ + 8, 8), :], (up, c)))

    def send_rim(ref, first, depth, sides=((-1, 0), (1, 0), (0, 1), (0, -1), (1, 1), (1, -1), (-1, 1), (-1, -1))):
        layer_spans = {1: (GL + 4 - depth, 4 - depth, depth), -1: (4, GL + 4, depth), 0: (4, 4, GL)}
        row_spans = {1: (first + CR - 4, first - 4, 4), -1: (first, first + CR, 4), 0: (first, first, CR)}
        copies = []
        for by_row, by_col in sides:
            from_layer, to_layer, count_layers = layer_spans[by_col]
            from_row, to_row, count_rows = row_spans[by_row]
            device = ((up, row, down)[by_row + 1], (left, col, right)[by_col + 1])
            copies.append(
                send(
                    ref.at[pl.ds(from_layer, count_layers), :, pl.ds(from_row, count_rows), :],
                    ref.at[pl.ds(to_layer, count_layers), :, pl.ds(to_row, count_rows), :],
                    device,
                )
            )
        return copies

    loaded(4, lat.at[pl.ds(4, GL), :, pl.ds(12, CR), :])
    loaded(5, ver.at[pl.ds(4, GL), :, pl.ds(4, CR), :])
    loaded(6, layers.at[:, pl.ds(8, CR), :])
    lat_copies = send_rim(lat, 12, 3)
    ver_copies = send_rim(ver, 4, 4)
    layer_copies = [
        send(layers.at[:, pl.ds(8, 8), :], layers.at[:, pl.ds(8 + CR, 8), :], (up, col)),
        send(layers.at[:, pl.ds(CR, 8), :], layers.at[:, pl.ds(0, 8), :], (down, col)),
    ]

    def pool_body(i, carry):
        r = lax.broadcasted_iota(jnp.int32, (128, 128), 0)
        c = lax.broadcasted_iota(jnp.int32, (128, 128), 1)
        start = pl.multiple_of(i * 128, 128)
        pool[pl.ds(start, 128), :] = jnp.where(16 * i + r // 8 == c, 1.0 / 64.0, 0.0).astype(BF16)
        spread[i] = jnp.where(16 * i + c // 8 == r, 1.0, 0.0).astype(BF16)
        return carry

    lax.fori_loop(0, NT, pool_body, 0)
    for index, (_, dst) in enumerate(power):
        loaded(7 + index, dst.at[pl.ds(1, NT - 2), pl.ds(16, TR), :])

    for copy in row_copies + col_copies:
        copy.wait_recv()
    has_up = jnp.where(row > 0, 1.0, 0.0).astype(F32)
    has_down = jnp.where(row < NR - 1, 1.0, 0.0).astype(F32)
    side_ok = jnp.logical_or(
        jnp.logical_and(lane < 64, col < NC - 1), jnp.logical_and(lane >= 64, col > 0)
    )
    for index, ref in enumerate((p_cond, p_dem, p_leak)):
        for t in range(NT):
            cut = slice(128 * t, 128 * t + 128)
            top = stage[0, index, :, cut]
            bottom = stage[1, index, :, cut]
            if index == 0:
                top, bottom = top * has_up, bottom * has_down
            ref[t, 8:16, :] = top
            ref[t, 16 + TR : 24 + TR, :] = bottom
    for t in range(NT):
        cut = slice(128 * t, 128 * t + 128)
        p_via[t, 8:16, :] = stage_i[0, :, cut]
        p_via[t, 16 + TR : 24 + TR, :] = stage_i[1, :, cut]

    def rim(a, q, from_right, from_left):
        at = 32 * q + 8 * a
        value = jnp.where(
            lane < 64,
            pltpu.roll(from_right, (128 - at) % 128, axis=1),
            pltpu.roll(from_left, (248 - at) % 128, axis=1),
        )
        if a == 0:
            return jnp.where(side_ok, value, 0.0)
        if a == 3:
            return value.astype(jnp.int32)
        return value

    def unpack_body(i, carry):
        base = pl.multiple_of(8 * i, 8)
        from_right = pl_recv[pl.ds(8 + base, 8), :]
        from_left = pr_recv[pl.ds(8 + base, 8), :]
        for a, ref in enumerate((p_cond, p_dem, p_leak, p_via)):
            for q in range(4):
                ref[NT, pl.ds(16 + q * TQ + base, 8), :] = rim(a, q, from_right, from_left)
        return carry

    lax.fori_loop(0, TQ // 8, unpack_body, 0)
    for a, ref in enumerate((p_cond, p_dem, p_leak, p_via)):
        top = rim(a, 3, pl_recv[0:8, :], pr_recv[0:8, :])
        bottom = rim(a, 0, pl_recv[TQ + 8 : TQ + 16, :], pr_recv[TQ + 8 : TQ + 16, :])
        if a == 0:
            top, bottom = top * has_up, bottom * has_down
        ref[NT, 8:16, :] = top
        ref[NT, 16 + TR : 24 + TR, :] = bottom

    last_tile = TR // 8 + 1

    def power_coefs(c_ref, with_load):
        def coef_tile(i):
            base = pl.multiple_of(8 + 8 * i, 8)
            row_ok = jnp.logical_and(
                jnp.logical_or(i > 0, row > 0), jnp.logical_or(i < last_tile, row < NR - 1)
            )
            rows = pl.ds(base, 8)
            centers = [c_ref[t, rows, :] for t in range(NT + 1)]
            west, east = west_east(centers)
            for t in range(NT + 1):
                c = centers[t]
                c_n = c + c_ref[t, pl.ds(base - 1, 8), :]
                c_s = c + c_ref[t, pl.ds(base + 1, 8), :]
                c_w = c + west[t]
                c_e = c + east[t]
                denom = 0.5 * ((c_n + c_s) + (c_w + c_e)) + VIA_CONDUCT * p_via[
                    t, rows, :
                ].astype(F32)
                ok = row_ok if t < NT else jnp.logical_and(side_ok, row_ok)
                inverse = jnp.where(ok, reciprocal(denom), 0.0)
                half = 0.5 * inverse
                a_n[t, rows, :] = c_n * half
                a_s[t, rows, :] = c_s * half
                a_w[t, rows, :] = c_w * half
                a_e[t, rows, :] = c_e * half
                if with_load:
                    value = p_dem[t, rows, :] + p_leak[t, rows, :]
                    load[t, rows, :] = value
                else:
                    value = load[t, rows, :]
                b_p[t, rows, :] = value * inverse

        def coef_body(j, carry):
            for k in range(COEF_TILES):
                coef_tile(COEF_TILES * j + k)
            return carry

        lax.fori_loop(0, pl.cdiv(TR // 8 + 2, COEF_TILES), coef_body, 0)

    def power_sweep(src, dst):
        per = (TR // 8 + 2) // HALVES

        def sweep_body(j, carry):
            for i in range(per):
                base = pl.multiple_of(8 + 8 * (per * j + i), 8)
                rows = pl.ds(base, 8)
                west, east = west_east([src[t, rows, :] for t in range(NT + 1)])
                for t in range(NT + 1):
                    dst[t, rows, :] = (
                        b_p[t, rows, :]
                        + a_n[t, rows, :] * src[t, pl.ds(base - 1, 8), :]
                        + a_s[t, rows, :] * src[t, pl.ds(base + 1, 8), :]
                    ) + (a_w[t, rows, :] * west[t] + a_e[t, rows, :] * east[t])
            return carry

        lax.fori_loop(0, HALVES, sweep_body, 0)

    def send_heat(c_ref, d_ref, work, phase):
        def heat_body(i, carry):
            for k in range(4):
                rows = pl.ds(pl.multiple_of(16 + 32 * i + 8 * k, 8), 8)
                for t in range(NT):
                    d = d_ref[t, rows, :]
                    work[t, rows, :] = load[t, rows, :] * (1.0 - d) + c_ref[t, rows, :] * d * d
                    if phase == 1:
                        out_rows = pl.ds(pl.multiple_of(32 * i + 8 * k, 8), 8)
                        drop_out[out_rows, 128 * t : 128 * t + 128] = d
            return carry

        lax.fori_loop(0, TR // 32, heat_body, 0)
        for j in range(CR // 8):
            for t in range(NT):
                total = work[t, pl.ds(16 + 64 * j, 8, stride=8), :]
                for k in range(1, 8):
                    total = total + work[t, pl.ds(16 + 64 * j + k, 8, stride=8), :]
                rows_sum[8 * j : 8 * j + 8, 128 * t : 128 * t + 128] = total
        heat = pooled(rows_sum[...], pool[...])
        heat_own[phase] = heat
        heat_all[phase, col, 8 : 8 + CR, :] = heat
        copies = [
            send(heat_own.at[phase], heat_all.at[phase, col, pl.ds(8, CR), :], (row, peer))
            for peer in peers
        ]
        for c in (col, *peers):
            for r, source, target in ((up, 0, 8 + CR), (down, CR - 8, 0)):
                copies.append(
                    send(
                        heat_own.at[phase, pl.ds(source, 8), :],
                        heat_all.at[phase, col, pl.ds(target, 8), :],
                        (r, c),
                    )
                )
        return copies

    tall = (CR + 8) // 8

    def thermal_coefs(place):
        low = jnp.logical_and(place == 3, col == 0)
        high = jnp.logical_and(place == GL + 2, col == NC - 1)
        for i in range(tall):
            rows = pl.ds(8 * i, 8)
            centers = [lat[place + 1, t, pl.ds(8 + 8 * i, 8), :] for t in range(NC)]
            west, east = west_east(centers)
            for t in range(NC):
                k, k_w, k_e = centers[t], west[t], east[t]
                k_n = lat[place + 1, t, pl.ds(7 + 8 * i, 8), :]
                k_s = lat[place + 1, t, pl.ds(9 + 8 * i, 8), :]
                v = ver[place + 1, t, rows, :]
                v_b = jnp.where(low, 0.0, ver[place, t, rows, :])
                v_a = jnp.where(high, 0.0, ver[place + 2, t, rows, :])
                edge_n = edge_s = edge_w = edge_e = None
                if i == 0:
                    edge_n = jnp.logical_and(sub == 4, row == 0)
                    k_n = jnp.where(edge_n, 0.0, k_n)
                if i == tall - 1:
                    edge_s = jnp.logical_and(sub == 3, row == NR - 1)
                    k_s = jnp.where(edge_s, 0.0, k_s)
                if t == 0:
                    edge_w = first_lane
                    k_w = jnp.where(edge_w, 0.0, k_w)
                if t == NC - 1:
                    edge_e = last_lane
                    k_e = jnp.where(edge_e, 0.0, k_e)
                sums = [k + k_n, k + k_s, k + k_w, k + k_e, v + v_b, v + v_a]
                twice = ((sums[0] + sums[1]) + (sums[2] + sums[3])) + (sums[4] + sums[5])
                inverse = reciprocal(twice)
                t_r[place, t, rows, :] = 2.0 * inverse
                edges = (edge_n, edge_s, edge_w, edge_e, low, high)
                for ref, total, edge in zip((t_n, t_s, t_w, t_e, t_b, t_a), sums, edges):
                    value = total * inverse
                    if edge is not None:
                        value = jnp.where(edge, 0.0, value)
                    ref[place, t, rows, :] = value

    def over(first, last, body):
        def over_body(j, carry):
            body(j)
            return carry

        lax.fori_loop(first, last, over_body, 0)

    def sources(phase, start):
        def source_layer(place):
            for i in range(tall):
                rows = pl.ds(8 * i, 8)
                near_rows = pl.ds(4 + 8 * i, 8)
                for t in range(NC):
                    here = layers[t, near_rows, :] == col * GL + place - 3
                    value = (
                        jnp.where(here, heat_all[phase, t, near_rows, :], 0.0)
                        * t_r[place, t, rows, :]
                    )
                    b_t[place, t, rows, :] = value
                    if start:
                        temp_0[place + 1, t, pl.ds(8 + 8 * i, 8), :] = value

        over(0, GL + 6, source_layer)

    def thermal_block(src, dst, first, depth):
        cache = {}

        def at(k, i, t):
            if (k, i, t) not in cache:
                cache[k, i, t] = src[first + k, t, pl.ds(8 + 8 * i, 8), :]
            return cache[k, i, t]

        for i in range(tall):
            rows = pl.ds(8 * i, 8)
            for k in range(depth):
                place = first + k
                plus = [pltpu.roll(at(k + 1, i, t), 1, axis=1) for t in range(NC)]
                minus = [pltpu.roll(at(k + 1, i, t), 127, axis=1) for t in range(NC)]
                for t in range(NC):
                    west = plus[t] if t == 0 else jnp.where(first_lane, plus[t - 1], plus[t])
                    east = minus[t] if t == NC - 1 else jnp.where(last_lane, minus[t + 1], minus[t])
                    dst[place + 1, t, pl.ds(8 + 8 * i, 8), :] = (
                        (
                            b_t[place, t, rows, :]
                            + t_n[place, t, rows, :] * src[place + 1, t, pl.ds(7 + 8 * i, 8), :]
                        )
                        + (
                            t_s[place, t, rows, :] * src[place + 1, t, pl.ds(9 + 8 * i, 8), :]
                            + t_b[place, t, rows, :] * at(k, i, t)
                        )
                        + (t_a[place, t, rows, :] * at(k + 2, i, t))
                        + (t_w[place, t, rows, :] * west + t_e[place, t, rows, :] * east)
                    )

    def thermal_sweep(src, dst, halo):
        over(
            0,
            GL // 2 + halo,
            lambda j: thermal_block(src, dst, 3 - halo + 2 * j, 2),
        )

    power_coefs(p_cond, True)
    power_sweep(b_p, d_0)
    power_sweep(d_0, d_1)
    power_sweep(d_1, d_0)
    heat_copies = send_heat(p_cond, d_0, d_1, 0)
    for copy in lat_copies + ver_copies:
        copy.wait_recv()
    over(0, GL + 6, thermal_coefs)
    for copy in heat_copies + layer_copies:
        copy.wait_recv()
    sources(0, True)
    pending = row_copies + col_copies + lat_copies + ver_copies + layer_copies + heat_copies
    thermal_sweep(temp_0, temp_1, 2)
    thermal_sweep(temp_1, temp_0, 1)
    thermal_sweep(temp_0, temp_1, 0)

    def part_body(i, carry):
        base = pl.multiple_of(8 * i, 8)
        for t in range(NC):
            ids = layers[t, pl.ds(8 + base, 8), :] - col * GL
            total = jnp.zeros((8, 128), F32)
            for layer in range(GL):
                total = jnp.where(
                    ids == layer, temp_1[layer + 4, t, pl.ds(12 + base, 8), :], total
                )
            part[t, pl.ds(base, 8), :] = total
        return carry

    lax.fori_loop(0, CR // 8, part_body, 0)
    part_copies = [
        send(part.at[peer], part_recv.at[k], (row, peer)) for k, peer in enumerate(peers)
    ]
    for copy in part_copies:
        copy.wait_recv()
    total = part[col]
    for k in range(NC - 1):
        total = total + part_recv[k]
    cell[1, 8 : 8 + CR, :] = total
    own = cell.at[1, pl.ds(8, CR), :]
    low_rows = cell.at[1, pl.ds(8, 8), :]
    high_rows = cell.at[1, pl.ds(CR, 8), :]
    above, below = pl.ds(0, 8), pl.ds(8 + CR, 8)
    cell_copies = [
        send(own, cell.at[0, pl.ds(8, CR), :], (row, right)),
        send(own, cell.at[2, pl.ds(8, CR), :], (row, left)),
    ]
    for place, c in ((1, col), (0, right), (2, left)):
        cell_copies.append(send(high_rows, cell.at[place, above, :], (down, c)))
        cell_copies.append(send(low_rows, cell.at[place, below, :], (up, c)))
    shapes = (
        (g_up, lambda x: reciprocal(1.0 + COND_SLOPE * x)),
        (e_up, lambda x: jnp.exp(LEAK_SLOPE * x)),
    )
    for target, shape in shapes:
        coarse = shape(total)
        for t in range(NT):
            target[t, 8 : 8 + CR, :] = pooled(coarse, spread[t])

    def warm_tile(i, tiles):
        rows = pl.ds(pl.multiple_of(8 + 8 * i, 8), 8)
        coarse = pl.ds(7 + i, 1)
        for t in tiles:
            c_now[t, rows, :] = p_cond[t, rows, :] * g_up[t, coarse, :]
            load[t, rows, :] = p_dem[t, rows, :] + p_leak[t, rows, :] * e_up[t, coarse, :]

    def warm_body(j, carry):
        for k in range(4):
            warm_tile(1 + 4 * j + k, range(NT))
        return carry

    lax.fori_loop(0, TR // 32, warm_body, 0)
    for copy in cell_copies:
        copy.wait_recv()
    for target, shape in shapes:
        coarse = shape(jnp.concatenate([cell[1, 0:8, :], cell[1, 8 + CR : 16 + CR, :]], axis=0))
        for t in range(NT):
            rims_up = pooled(coarse, spread[t])
            target[t, 0:8, :] = rims_up[0:8]
            target[t, 8 + CR : 16 + CR, :] = rims_up[8:16]
        from_left = jnp.broadcast_to(shape(cell[0])[:, 127:128], (CR + 16, 128))
        from_right = jnp.broadcast_to(shape(cell[2])[:, 0:1], (CR + 16, 128))
        wide = lax.broadcasted_iota(jnp.int32, (CR + 16, 128), 1)
        target[NT] = jnp.where(wide < 64, from_right, from_left)
    warm_tile(0, range(NT))
    warm_tile(last_tile, range(NT))

    def warm_side_body(j, carry):
        for k in range(2):
            warm_tile(2 * j + k, (NT,))
        return carry

    lax.fori_loop(0, TR // 16 + 1, warm_side_body, 0)

    temp_copies = send_rim(temp_1, 12, 4)
    power_coefs(c_now, False)
    power_sweep(d_0, d_1)
    power_sweep(d_1, d_0)
    power_sweep(d_0, d_1)
    power_sweep(d_1, d_0)
    heat_copies = send_heat(c_now, d_0, d_1, 1)
    for copy in heat_copies:
        copy.wait_recv()
    sources(1, False)
    for copy in temp_copies:
        copy.wait()
    thermal_sweep(temp_1, temp_0, 3)
    thermal_sweep(temp_0, temp_1, 2)
    thermal_sweep(temp_1, temp_0, 1)
    thermal_sweep(temp_0, temp_1, 0)
    for t in range(NC):
        pltpu.make_async_copy(
            temp_1.at[pl.ds(4, GL), t, pl.ds(12, CR), :],
            temp_out.at[:, :, pl.ds(128 * t, 128)],
            load_sem.at[11],
        ).start()
    for copy in pending + part_copies + cell_copies + heat_copies:
        copy.wait_send()
    loaded(11, temp_1.at[pl.ds(4, GL), :, pl.ds(12, CR), :])


def body(num_rows, num_cols, demand, leakage, conductance, vias, layer_of, lateral_k, vertical_k):
    tile_rows, tile_cols = demand.shape
    group_layers, cell_rows, therm_cols = lateral_k.shape
    sizes = (num_rows, num_cols, tile_rows, group_layers, cell_rows)
    fine = pltpu.VMEM((9, tile_rows + 48, 128), F32)
    slab = pltpu.VMEM((group_layers + 6, num_cols, cell_rows + 8, 128), F32)
    coarse = (cell_rows, 128)
    hbm = pl.BlockSpec(memory_space=pl.ANY)
    return pl.pallas_call(
        functools.partial(kernel, sizes),
        out_shape=(
            jax.ShapeDtypeStruct(demand.shape, F32),
            jax.ShapeDtypeStruct(lateral_k.shape, F32),
        ),
        in_specs=[hbm] * 7,
        out_specs=(pl.BlockSpec(memory_space=pltpu.VMEM), hbm),
        scratch_shapes=[fine] * 3
        + [pltpu.VMEM((9, tile_rows + 48, 128), jnp.int32)]
        + [fine] * 9
        + [
            pltpu.VMEM((2, 3, 8, tile_cols), F32),
            pltpu.VMEM((2, 8, tile_cols), jnp.int32),
            pltpu.VMEM((tile_rows // 4, 128), F32),
            pltpu.VMEM((tile_rows // 4, 128), F32),
            pltpu.VMEM((tile_rows // 4 + 16, 128), F32),
            pltpu.VMEM((tile_rows // 4 + 16, 128), F32),
            pltpu.VMEM((num_cols, cell_rows + 16, 128), jnp.int32),
            pltpu.VMEM((group_layers + 8, num_cols, cell_rows + 24, 128), F32),
            pltpu.VMEM((group_layers + 8, num_cols, cell_rows + 8, 128), F32),
        ]
        + [slab] * 8
        + [
            pltpu.VMEM((group_layers + 8, num_cols, cell_rows + 24, 128), F32),
            pltpu.VMEM((group_layers + 8, num_cols, cell_rows + 24, 128), F32),
            pltpu.VMEM((tile_cols, 128), BF16),
            pltpu.VMEM((8, 128, 128), BF16),
            pltpu.VMEM((cell_rows, tile_cols), F32),
            pltpu.VMEM((2,) + coarse, F32),
            pltpu.VMEM((2, num_cols, cell_rows + 16, 128), F32),
            pltpu.VMEM((num_cols,) + coarse, F32),
            pltpu.VMEM((num_cols - 1,) + coarse, F32),
            pltpu.VMEM((3, cell_rows + 16, 128), F32),
            pltpu.VMEM((9, cell_rows + 16, 128), F32),
            pltpu.VMEM((9, cell_rows + 16, 128), F32),
            pltpu.SemaphoreType.DMA((12,)),
            pltpu.SemaphoreType.DMA((LINKS,)),
            pltpu.SemaphoreType.DMA((LINKS,)),
        ],
        compiler_params=pltpu.CompilerParams(
            collective_id=0, has_side_effects=True, vmem_limit_bytes=58 << 20
        ),
        name="coupled",
    )(demand, leakage, conductance, vias, layer_of, lateral_k, vertical_k)


def solution(mesh):
    in_specs = (
        P("row", "col"),
        P("row", "col"),
        P("row", "col"),
        P("row", "col"),
        P("row", None),
        P("col", "row", None),
        P("col", "row", None),
    )
    out_specs = (P("row", "col"), P("col", "row", None))
    step = functools.partial(body, mesh.shape["row"], mesh.shape["col"])
    return jax.shard_map(step, mesh=mesh, in_specs=in_specs, out_specs=out_specs, check_vma=False)
```

```python
import functools

import jax
import jax.numpy as jnp
from jax import lax
from jax.experimental import pallas as pl
from jax.experimental.pallas import tpu as pltpu
from jax.sharding import PartitionSpec as P

COARSE = 8
SWEEPS = 4
HEAT_SWEEPS = 4
COND_SLOPE = 0.5
LEAK_SLOPE = 0.7
VIA_CONDUCT = 4.0

MESH = pl.DeviceIdType.MESH
F32 = jnp.float32
BF16 = jnp.bfloat16
LINKS = 160
COEF_TILES = 4
HALVES = 2


def reciprocal(value):
    return 1.0 / value


def pooled(left, right):
    parts = []
    for _ in range(3):
        part = left.astype(BF16).astype(F32)
        parts.append(part)
        left = left - part
    count = left.shape[0]
    stacked = jnp.concatenate(parts, axis=0).astype(BF16)
    product = jnp.dot(stacked, right, preferred_element_type=F32)
    return (product[2 * count :] + product[count : 2 * count]) + product[:count]


def kernel(
    sizes,
    demand,
    leakage,
    conductance,
    vias,
    layer_of,
    lateral,
    vertical,
    drop_out,
    temp_out,
    p_cond,
    p_dem,
    p_leak,
    p_via,
    c_now,
    load,
    a_n,
    a_s,
    a_w,
    a_e,
    b_p,
    d_0,
    d_1,
    stage,
    stage_i,
    pl_send,
    pr_send,
    pl_recv,
    pr_recv,
    layers,
    lat,
    ver,
    t_n,
    t_s,
    t_w,
    t_e,
    t_b,
    t_a,
    t_r,
    b_t,
    r_far,
    temp_0,
    temp_1,
    pool,
    spread,
    rows_sum,
    rim_send,
    rim_recv,
    face_send,
    face_recv,
    heat_own,
    heat_all,
    part,
    part_recv,
    cell,
    g_up,
    e_up,
    load_sem,
    send_sem,
    recv_sem,
):
    NR, NC, TR, GL, CR = sizes
    NT = 8
    TQ = TR // 4
    row = lax.axis_index("row")
    col = lax.axis_index("col")
    up, down = lax.rem(row + NR - 1, NR), lax.rem(row + 1, NR)
    left, right = lax.rem(col + NC - 1, NC), lax.rem(col + 1, NC)
    peers = [lax.rem(col + k, NC) for k in range(1, NC)]
    count = [0]

    def send(src, dst, device):
        slot = count[0]
        count[0] += 1
        copy = pltpu.make_async_remote_copy(
            src_ref=src,
            dst_ref=dst,
            send_sem=send_sem.at[slot],
            recv_sem=recv_sem.at[slot],
            device_id=device,
            device_id_type=MESH,
        )
        copy.start()
        return copy

    lane = lax.broadcasted_iota(jnp.int32, (8, 128), 1)
    sub = lax.broadcasted_iota(jnp.int32, (8, 128), 0)
    first_lane = lane == 0
    last_lane = lane == 127

    def west_east(tiles):
        n = len(tiles)
        plus = [pltpu.roll(x, 1, axis=1) for x in tiles]
        minus = [pltpu.roll(x, 127, axis=1) for x in tiles]
        west = [jnp.where(first_lane, plus[t - 1], plus[t]) for t in range(n)]
        east = [jnp.where(last_lane, minus[(t + 1) % n], minus[t]) for t in range(n)]
        return west, east

    barrier = pltpu.get_barrier_semaphore()
    near = [(row, p) for p in peers]
    near += [(r, c) for r in (up, down) for c in (col, left, right)]
    for device in near:
        pl.semaphore_signal(barrier, inc=1, device_id=device, device_id_type=MESH)

    power = ((conductance, p_cond), (demand, p_dem), (leakage, p_leak), (vias, p_via))
    outer_tiles, inner_tiles = (0, NT - 1), tuple(range(1, NT - 1))
    for offset, tiles in ((0, outer_tiles), (7, inner_tiles)):
        for index, (src, dst) in enumerate(power):
            for t in tiles:
                pltpu.make_async_copy(
                    src.at[:, pl.ds(128 * t, 128)],
                    dst.at[t, pl.ds(16, TR), :],
                    load_sem.at[offset + index],
                ).start()
    for t in range(NC):
        cut = pl.ds(128 * t, 128)
        pltpu.make_async_copy(
            lateral.at[:, :, cut], lat.at[:, t, pl.ds(8, CR), :], load_sem.at[4]
        ).start()
        pltpu.make_async_copy(
            vertical.at[:, :, cut], ver.at[pl.ds(1, GL), t], load_sem.at[5]
        ).start()
        pltpu.make_async_copy(layer_of.at[:, cut], layers.at[t], load_sem.at[6]).start()

    def loaded(index, ref):
        pltpu.make_async_copy(ref, ref, load_sem.at[index]).wait()

    for index, (_, dst) in enumerate(power):
        loaded(index, dst.at[pl.ds(0, 2), pl.ds(16, TR), :])

    def pack_body(i, carry):
        base = pl.multiple_of(8 * i, 8)
        acc_l = acc_r = jnp.zeros((8, 128), F32)
        for q in range(4):
            for a, ref in enumerate((p_cond, p_dem, p_leak, p_via)):
                at = 32 * q + 8 * a
                rows = pl.ds(16 + q * TQ + base, 8)
                lo = ref[0, rows, :].astype(F32)
                hi = ref[NT - 1, rows, :].astype(F32)
                here = lane // 8 == at // 8
                acc_l = jnp.where(here, pltpu.roll(lo, at, axis=1), acc_l)
                acc_r = jnp.where(here, pltpu.roll(hi, (at + 8) % 128, axis=1), acc_r)
        pl_send[pl.ds(base, 8), :] = acc_l
        pr_send[pl.ds(base, 8), :] = acc_r
        return carry

    lax.fori_loop(0, TQ // 8, pack_body, 0)
    pl.semaphore_wait(barrier, len(near))

    row_copies = []
    for index, src in enumerate((conductance, demand, leakage, vias)):
        for side, start, device in ((0, TR - 8, (down, col)), (1, 0, (up, col))):
            dst = stage_i.at[side] if index == 3 else stage.at[side, index]
            row_copies.append(send(src.at[pl.ds(start, 8), :], dst, device))

    col_copies = []
    for src, dst, c in ((pl_send, pl_recv, left), (pr_send, pr_recv, right)):
        col_copies.append(send(src, dst.at[pl.ds(8, TQ), :], (row, c)))
        col_copies.append(send(src.at[pl.ds(TQ - 8, 8), :], dst.at[pl.ds(0, 8), :], (down, c)))
        col_copies.append(send(src.at[pl.ds(0, 8), :], dst.at[pl.ds(TQ + 8, 8), :], (up, c)))

    def send_rows(ref, first):
        span = pl.ds(first, GL)
        return [
            send(
                ref.at[span, :, pl.ds(8, 1), :], ref.at[span, :, pl.ds(8 + CR, 1), :], (up, col)
            ),
            send(
                ref.at[span, :, pl.ds(7 + CR, 1), :], ref.at[span, :, pl.ds(7, 1), :], (down, col)
            ),
        ]

    loaded(4, lat.at[:, :, pl.ds(8, CR), :])
    lat_copies = send_rows(lat, 0)
    ver_copies = []
    for t in range(NC):
        cut = pl.ds(128 * t, 128)
        ver_copies.append(send(vertical.at[GL - 1, :, cut], ver.at[0, t], (row, right)))
        ver_copies.append(send(vertical.at[0, :, cut], ver.at[GL + 1, t], (row, left)))

    def pool_body(i, carry):
        r = lax.broadcasted_iota(jnp.int32, (128, 128), 0)
        c = lax.broadcasted_iota(jnp.int32, (128, 128), 1)
        start = pl.multiple_of(i * 128, 128)
        pool[pl.ds(start, 128), :] = jnp.where(16 * i + r // 8 == c, 1.0 / 64.0, 0.0).astype(BF16)
        spread[i] = jnp.where(16 * i + c // 8 == r, 1.0, 0.0).astype(BF16)
        return carry

    lax.fori_loop(0, NT, pool_body, 0)
    for index, (_, dst) in enumerate(power):
        loaded(7 + index, dst.at[pl.ds(1, NT - 2), pl.ds(16, TR), :])

    for copy in row_copies + col_copies:
        copy.wait_recv()
    has_up = jnp.where(row > 0, 1.0, 0.0).astype(F32)
    has_down = jnp.where(row < NR - 1, 1.0, 0.0).astype(F32)
    side_ok = jnp.logical_or(
        jnp.logical_and(lane < 64, col < NC - 1), jnp.logical_and(lane >= 64, col > 0)
    )
    for index, ref in enumerate((p_cond, p_dem, p_leak)):
        for t in range(NT):
            cut = slice(128 * t, 128 * t + 128)
            top = stage[0, index, :, cut]
            bottom = stage[1, index, :, cut]
            if index == 0:
                top, bottom = top * has_up, bottom * has_down
            ref[t, 8:16, :] = top
            ref[t, 16 + TR : 24 + TR, :] = bottom
    for t in range(NT):
        cut = slice(128 * t, 128 * t + 128)
        p_via[t, 8:16, :] = stage_i[0, :, cut]
        p_via[t, 16 + TR : 24 + TR, :] = stage_i[1, :, cut]

    def rim(a, q, from_right, from_left):
        at = 32 * q + 8 * a
        value = jnp.where(
            lane < 64,
            pltpu.roll(from_right, (128 - at) % 128, axis=1),
            pltpu.roll(from_left, (248 - at) % 128, axis=1),
        )
        if a == 0:
            return jnp.where(side_ok, value, 0.0)
        if a == 3:
            return value.astype(jnp.int32)
        return value

    def unpack_body(i, carry):
        base = pl.multiple_of(8 * i, 8)
        from_right = pl_recv[pl.ds(8 + base, 8), :]
        from_left = pr_recv[pl.ds(8 + base, 8), :]
        for a, ref in enumerate((p_cond, p_dem, p_leak, p_via)):
            for q in range(4):
                ref[NT, pl.ds(16 + q * TQ + base, 8), :] = rim(a, q, from_right, from_left)
        return carry

    lax.fori_loop(0, TQ // 8, unpack_body, 0)
    for a, ref in enumerate((p_cond, p_dem, p_leak, p_via)):
        top = rim(a, 3, pl_recv[0:8, :], pr_recv[0:8, :])
        bottom = rim(a, 0, pl_recv[TQ + 8 : TQ + 16, :], pr_recv[TQ + 8 : TQ + 16, :])
        if a == 0:
            top, bottom = top * has_up, bottom * has_down
        ref[NT, 8:16, :] = top
        ref[NT, 16 + TR : 24 + TR, :] = bottom

    last_tile = TR // 8 + 1

    def power_coefs(c_ref, with_load):
        def coef_tile(i):
            base = pl.multiple_of(8 + 8 * i, 8)
            row_ok = jnp.logical_and(
                jnp.logical_or(i > 0, row > 0), jnp.logical_or(i < last_tile, row < NR - 1)
            )
            rows = pl.ds(base, 8)
            centers = [c_ref[t, rows, :] for t in range(NT + 1)]
            west, east = west_east(centers)
            for t in range(NT + 1):
                c = centers[t]
                c_n = c + c_ref[t, pl.ds(base - 1, 8), :]
                c_s = c + c_ref[t, pl.ds(base + 1, 8), :]
                c_w = c + west[t]
                c_e = c + east[t]
                denom = 0.5 * ((c_n + c_s) + (c_w + c_e)) + VIA_CONDUCT * p_via[
                    t, rows, :
                ].astype(F32)
                ok = row_ok if t < NT else jnp.logical_and(side_ok, row_ok)
                inverse = jnp.where(ok, reciprocal(denom), 0.0)
                half = 0.5 * inverse
                a_n[t, rows, :] = c_n * half
                a_s[t, rows, :] = c_s * half
                a_w[t, rows, :] = c_w * half
                a_e[t, rows, :] = c_e * half
                if with_load:
                    value = p_dem[t, rows, :] + p_leak[t, rows, :]
                    load[t, rows, :] = value
                else:
                    value = load[t, rows, :]
                b_p[t, rows, :] = value * inverse

        def coef_body(j, carry):
            for k in range(COEF_TILES):
                coef_tile(COEF_TILES * j + k)
            return carry

        lax.fori_loop(0, pl.cdiv(TR // 8 + 2, COEF_TILES), coef_body, 0)

    def power_sweep(src, dst):
        per = (TR // 8 + 2) // HALVES

        def sweep_body(j, carry):
            for i in range(per):
                base = pl.multiple_of(8 + 8 * (per * j + i), 8)
                rows = pl.ds(base, 8)
                west, east = west_east([src[t, rows, :] for t in range(NT + 1)])
                for t in range(NT + 1):
                    dst[t, rows, :] = (
                        b_p[t, rows, :]
                        + a_n[t, rows, :] * src[t, pl.ds(base - 1, 8), :]
                        + a_s[t, rows, :] * src[t, pl.ds(base + 1, 8), :]
                    ) + (a_w[t, rows, :] * west[t] + a_e[t, rows, :] * east[t])
            return carry

        lax.fori_loop(0, HALVES, sweep_body, 0)

    def send_heat(c_ref, d_ref, work, phase):
        def heat_body(i, carry):
            for k in range(4):
                rows = pl.ds(pl.multiple_of(16 + 32 * i + 8 * k, 8), 8)
                for t in range(NT):
                    d = d_ref[t, rows, :]
                    work[t, rows, :] = load[t, rows, :] * (1.0 - d) + c_ref[t, rows, :] * d * d
                    if phase == 1:
                        out_rows = pl.ds(pl.multiple_of(32 * i + 8 * k, 8), 8)
                        drop_out[out_rows, 128 * t : 128 * t + 128] = d
            return carry

        lax.fori_loop(0, TR // 32, heat_body, 0)
        for j in range(CR // 8):
            for t in range(NT):
                total = work[t, pl.ds(16 + 64 * j, 8, stride=8), :]
                for k in range(1, 8):
                    total = total + work[t, pl.ds(16 + 64 * j + k, 8, stride=8), :]
                rows_sum[8 * j : 8 * j + 8, 128 * t : 128 * t + 128] = total
        heat = pooled(rows_sum[...], pool[...])
        heat_own[phase] = heat
        heat_all[phase, col] = heat
        return [
            send(heat_own.at[phase], heat_all.at[phase, col], (row, peer)) for peer in peers
        ]

    def thermal_coefs(layer):
        low = jnp.logical_and(layer == 0, col == 0)
        high = jnp.logical_and(layer == GL - 1, col == NC - 1)
        for i in range(CR // 8):
            rows = pl.ds(8 * i, 8)
            centers = [lat[layer, t, pl.ds(8 + 8 * i, 8), :] for t in range(NC)]
            west, east = west_east(centers)
            for t in range(NC):
                k, k_w, k_e = centers[t], west[t], east[t]
                k_n = lat[layer, t, pl.ds(7 + 8 * i, 8), :]
                k_s = lat[layer, t, pl.ds(9 + 8 * i, 8), :]
                v = ver[layer + 1, t, rows, :]
                v_b = jnp.where(low, 0.0, ver[layer, t, rows, :])
                v_a = jnp.where(high, 0.0, ver[layer + 2, t, rows, :])
                edge_n = edge_s = edge_w = edge_e = None
                if i == 0:
                    edge_n = jnp.logical_and(sub == 0, row == 0)
                    k_n = jnp.where(edge_n, 0.0, k_n)
                if i == CR // 8 - 1:
                    edge_s = jnp.logical_and(sub == 7, row == NR - 1)
                    k_s = jnp.where(edge_s, 0.0, k_s)
                if t == 0:
                    edge_w = first_lane
                    k_w = jnp.where(edge_w, 0.0, k_w)
                if t == NC - 1:
                    edge_e = last_lane
                    k_e = jnp.where(edge_e, 0.0, k_e)
                sums = [k + k_n, k + k_s, k + k_w, k + k_e, v + v_b, v + v_a]
                twice = ((sums[0] + sums[1]) + (sums[2] + sums[3])) + (sums[4] + sums[5])
                inverse = reciprocal(twice)
                t_r[layer, t, rows, :] = 2.0 * inverse
                edges = (edge_n, edge_s, edge_w, edge_e, low, high)
                for ref, total, edge in zip((t_n, t_s, t_w, t_e, t_b, t_a), sums, edges):
                    value = total * inverse
                    if edge is not None:
                        value = jnp.where(edge, 0.0, value)
                    ref[layer, t, rows, :] = value

    def sources(phase, start):
        def source_body(layer, carry):
            for i in range(CR // 8):
                rows = pl.ds(8 * i, 8)
                for t in range(NC):
                    here = layers[t, rows, :] == col * GL + layer
                    value = (
                        jnp.where(here, heat_all[phase, t, rows, :], 0.0) * t_r[layer, t, rows, :]
                    )
                    b_t[layer, t, rows, :] = value
                    if start:
                        temp_0[layer + 1, t, pl.ds(8 + 8 * i, 8), :] = value
            return carry

        lax.fori_loop(0, GL, source_body, 0)
        if start:
            for side, target, layer in ((0, 0, -1), (1, GL + 1, GL)):
                for i in range(CR // 8):
                    rows = pl.ds(8 * i, 8)
                    for t in range(NC):
                        here = layers[t, rows, :] == col * GL + layer
                        temp_0[target, t, pl.ds(8 + 8 * i, 8), :] = (
                            jnp.where(here, heat_all[phase, t, rows, :], 0.0)
                            * r_far[side, t, rows, :]
                        )

    half = NC // 2
    chunks = (range(half), range(half, NC))
    tall = CR // 8
    edge_tiles = sorted({0, tall - 1})
    mid_tiles = [i for i in range(tall) if i not in edge_tiles]

    def thermal_block(src, dst, first, depth, row_tiles, tiles, out=None):
        cache = {}

        def at(k, i, t):
            if (k, i, t) not in cache:
                cache[k, i, t] = src[first + k, t, pl.ds(8 + 8 * i, 8), :]
            return cache[k, i, t]

        for k in range(depth):
            layer = first + k
            for i in row_tiles:
                rows = pl.ds(8 * i, 8)
                plus = {
                    t: pltpu.roll(at(k + 1, i, t), 1, axis=1)
                    for t in range(max(tiles[0] - 1, 0), tiles[-1] + 1)
                }
                minus = {
                    t: pltpu.roll(at(k + 1, i, t), 127, axis=1)
                    for t in range(tiles[0], min(tiles[-1] + 2, NC))
                }
                for t in tiles:
                    west = plus[t] if t == 0 else jnp.where(first_lane, plus[t - 1], plus[t])
                    east = minus[t] if t == NC - 1 else jnp.where(last_lane, minus[t + 1], minus[t])
                    value = (
                        (
                            b_t[layer, t, rows, :]
                            + t_n[layer, t, rows, :] * src[layer + 1, t, pl.ds(7 + 8 * i, 8), :]
                        )
                        + (
                            t_s[layer, t, rows, :] * src[layer + 1, t, pl.ds(9 + 8 * i, 8), :]
                            + t_b[layer, t, rows, :] * at(k, i, t)
                        )
                        + (t_a[layer, t, rows, :] * at(k + 2, i, t))
                        + (t_w[layer, t, rows, :] * west + t_e[layer, t, rows, :] * east)
                    )
                    if out is None:
                        dst[layer + 1, t, pl.ds(8 + 8 * i, 8), :] = value
                    else:
                        out[layer, rows, 128 * t : 128 * t + 128] = value

    def inner_layers(src, dst, row_tiles, out=None):
        depth = (GL - 2) // 2

        def inner_body(j, carry):
            thermal_block(src, dst, 1 + depth * j, depth, row_tiles, range(NC), out)
            return carry

        if row_tiles:
            lax.fori_loop(0, 2, inner_body, 0)

    def send_planes(ref, chunk):
        mid, tiles = pl.ds(8, CR), pl.ds(chunk[0], len(chunk))
        return [
            send(ref.at[GL, tiles, mid, :], ref.at[0, tiles, mid, :], (row, right)),
            send(ref.at[1, tiles, mid, :], ref.at[GL + 1, tiles, mid, :], (row, left)),
        ]

    def copy_rims(ref, level, layer_list, tiles, buffer, place, put):
        for layer, slot in layer_list:
            for t in tiles:
                for side, inside, outside in ((0, 8, 8 + CR), (1, 7 + CR, 7)):
                    if put:
                        ref[layer + 1, t, pl.ds(outside, 1), :] = buffer[place(side, t, slot)]
                    else:
                        buffer[place(side, t, slot)] = ref[layer + 1, t, pl.ds(inside, 1), :]

    def inner_rims(ref, level, buffer, put):
        def rim_body(layer, carry):
            copy_rims(
                ref,
                level,
                ((layer, layer),),
                range(NC),
                buffer,
                lambda side, t, slot: (level - 1, side, t, pl.ds(slot, 1), slice(None)),
                put,
            )
            return carry

        lax.fori_loop(1, GL - 1, rim_body, 0)

    def face_rims(ref, level, index, buffer, put):
        copy_rims(
            ref,
            level,
            ((0, 0), (GL - 1, 1)),
            chunks[index],
            buffer,
            lambda side, t, slot: (
                level - 1,
                side,
                index,
                t - chunks[index][0],
                pl.ds(slot, 1),
                slice(None),
            ),
            put,
        )

    def send_inner(ref, level):
        inner_rims(ref, level, rim_send, False)
        return [
            send(rim_send.at[level - 1, side], rim_recv.at[level - 1, side], (r, col))
            for side, r in ((0, up), (1, down))
        ]

    def send_face(ref, level, index):
        face_rims(ref, level, index, face_send, False)
        cut = pl.ds(0, 2)
        return [
            send(
                face_send.at[level - 1, side, index, :, cut, :],
                face_recv.at[level - 1, side, index, :, cut, :],
                (r, col),
            )
            for side, r in ((0, up), (1, down))
        ]

    def faces(body):
        def face_body(j, carry):
            body(j * (GL - 1))
            return carry

        lax.fori_loop(0, 2, face_body, 0)

    def interior(body):
        def interior_body(j, carry):
            body(j)
            return carry

        lax.fori_loop(1, GL - 1, interior_body, 0)

    power_coefs(p_cond, True)
    loaded(5, ver.at[pl.ds(1, GL)])
    loaded(6, layers)
    for copy in ver_copies + lat_copies:
        copy.wait_recv()
    faces(thermal_coefs)
    r_copies = [
        send(t_r.at[GL - 1], r_far.at[0], (row, right)),
        send(t_r.at[0], r_far.at[1], (row, left)),
    ]
    power_sweep(b_p, d_0)
    power_sweep(d_0, d_1)
    power_sweep(d_1, d_0)
    heat_copies = send_heat(p_cond, d_0, d_1, 0)
    interior(thermal_coefs)
    for copy in heat_copies + r_copies:
        copy.wait_recv()
    sources(0, True)
    pending = list(row_copies + col_copies + ver_copies + lat_copies + r_copies + heat_copies)

    face_copies = {1: [send_face(temp_0, 1, index) for index in range(2)]}
    rims = {1: send_inner(temp_0, 1)}
    planes = {}

    def sweep(level, exchange=True, out=None):
        src, dst = (temp_0, temp_1) if level % 2 == 0 else (temp_1, temp_0)
        for copies in planes.get(level - 2, ()):
            for copy in copies:
                copy.wait_send()
        planes_now, faces_now = [], []
        for index, chunk in enumerate(chunks):
            for copy in face_copies[level - 1][index]:
                copy.wait_recv()
            if level - 1 in planes:
                for copy in planes[level - 1][index]:
                    copy.wait_recv()
            face_rims(src, level - 1, index, face_recv, True)
            for layer in (0, GL - 1):
                thermal_block(src, dst, layer, 1, range(tall), chunk, out)
            if exchange:
                planes_now.append(send_planes(dst, chunk))
                faces_now.append(send_face(dst, level, index))
        for copy in rims[level - 1]:
            copy.wait_recv()
        inner_rims(src, level - 1, rim_recv, True)
        if exchange:
            planes[level], face_copies[level] = planes_now, faces_now
            inner_layers(src, dst, edge_tiles)
            rims[level] = send_inner(dst, level)
            inner_layers(src, dst, mid_tiles)
        else:
            inner_layers(src, dst, list(range(tall)), out)

    sweep(2)
    sweep(3)
    sweep(4, False)

    def part_body(i, carry):
        base = pl.multiple_of(8 * i, 8)
        for t in range(NC):
            ids = layers[t, pl.ds(base, 8), :] - col * GL
            total = jnp.zeros((8, 128), F32)
            for layer in range(GL):
                total = jnp.where(
                    ids == layer, temp_1[layer + 1, t, pl.ds(8 + base, 8), :], total
                )
            part[t, pl.ds(base, 8), :] = total
        return carry

    lax.fori_loop(0, CR // 8, part_body, 0)
    part_copies = [
        send(part.at[peer], part_recv.at[k], (row, peer)) for k, peer in enumerate(peers)
    ]
    for copy in part_copies:
        copy.wait_recv()
    total = part[col]
    for k in range(NC - 1):
        total = total + part_recv[k]
    cell[1, 8 : 8 + CR, :] = total
    own = cell.at[1, pl.ds(8, CR), :]
    low_rows = cell.at[1, pl.ds(8, 8), :]
    high_rows = cell.at[1, pl.ds(CR, 8), :]
    above, below = pl.ds(0, 8), pl.ds(8 + CR, 8)
    cell_copies = [
        send(own, cell.at[0, pl.ds(8, CR), :], (row, right)),
        send(own, cell.at[2, pl.ds(8, CR), :], (row, left)),
    ]
    for place, c in ((1, col), (0, right), (2, left)):
        cell_copies.append(send(high_rows, cell.at[place, above, :], (down, c)))
        cell_copies.append(send(low_rows, cell.at[place, below, :], (up, c)))
    shapes = (
        (g_up, lambda x: reciprocal(1.0 + COND_SLOPE * x)),
        (e_up, lambda x: jnp.exp(LEAK_SLOPE * x)),
    )
    for target, shape in shapes:
        coarse = shape(total)
        for t in range(NT):
            target[t, 8 : 8 + CR, :] = pooled(coarse, spread[t])

    def warm_tile(i, tiles):
        rows = pl.ds(pl.multiple_of(8 + 8 * i, 8), 8)
        coarse = pl.ds(7 + i, 1)
        for t in tiles:
            c_now[t, rows, :] = p_cond[t, rows, :] * g_up[t, coarse, :]
            load[t, rows, :] = p_dem[t, rows, :] + p_leak[t, rows, :] * e_up[t, coarse, :]

    def warm_body(j, carry):
        for k in range(4):
            warm_tile(1 + 4 * j + k, range(NT))
        return carry

    lax.fori_loop(0, TR // 32, warm_body, 0)
    for copy in cell_copies:
        copy.wait_recv()
    for target, shape in shapes:
        coarse = shape(jnp.concatenate([cell[1, 0:8, :], cell[1, 8 + CR : 16 + CR, :]], axis=0))
        for t in range(NT):
            rims_up = pooled(coarse, spread[t])
            target[t, 0:8, :] = rims_up[0:8]
            target[t, 8 + CR : 16 + CR, :] = rims_up[8:16]
        from_left = jnp.broadcast_to(shape(cell[0])[:, 127:128], (CR + 16, 128))
        from_right = jnp.broadcast_to(shape(cell[2])[:, 0:1], (CR + 16, 128))
        wide = lax.broadcasted_iota(jnp.int32, (CR + 16, 128), 1)
        target[NT] = jnp.where(wide < 64, from_right, from_left)
    warm_tile(0, range(NT))
    warm_tile(last_tile, range(NT))

    def warm_side_body(j, carry):
        for k in range(2):
            warm_tile(2 * j + k, (NT,))
        return carry

    lax.fori_loop(0, TR // 16 + 1, warm_side_body, 0)

    planes[4] = [send_planes(temp_1, chunk) for chunk in chunks]
    face_copies[4] = [send_face(temp_1, 4, index) for index in range(2)]
    rims[4] = send_inner(temp_1, 4)
    power_coefs(c_now, False)
    power_sweep(d_0, d_1)
    power_sweep(d_1, d_0)
    power_sweep(d_0, d_1)
    power_sweep(d_1, d_0)
    heat_copies = send_heat(c_now, d_0, d_1, 1)
    for copy in heat_copies:
        copy.wait_recv()
    sources(1, False)
    pending += part_copies + cell_copies + heat_copies
    sweep(5)
    sweep(6)
    sweep(7)
    sweep(8, False, temp_out)
    for copies in rims.values():
        pending += copies
    for pair in face_copies.values():
        for copies in pair:
            pending += copies
    for copies in planes[7]:
        pending += copies
    for copy in pending:
        copy.wait_send()


def body(num_rows, num_cols, demand, leakage, conductance, vias, layer_of, lateral_k, vertical_k):
    tile_rows, tile_cols = demand.shape
    group_layers, cell_rows, therm_cols = lateral_k.shape
    sizes = (num_rows, num_cols, tile_rows, group_layers, cell_rows)
    fine = pltpu.VMEM((9, tile_rows + 48, 128), F32)
    slab = pltpu.VMEM((group_layers, num_cols, cell_rows, 128), F32)
    coarse = (cell_rows, 128)
    hbm = pl.BlockSpec(memory_space=pl.ANY)
    return pl.pallas_call(
        functools.partial(kernel, sizes),
        out_shape=(
            jax.ShapeDtypeStruct(demand.shape, F32),
            jax.ShapeDtypeStruct(lateral_k.shape, F32),
        ),
        in_specs=[hbm] * 7,
        out_specs=(pl.BlockSpec(memory_space=pltpu.VMEM),) * 2,
        scratch_shapes=[fine] * 3
        + [pltpu.VMEM((9, tile_rows + 48, 128), jnp.int32)]
        + [fine] * 9
        + [
            pltpu.VMEM((2, 3, 8, tile_cols), F32),
            pltpu.VMEM((2, 8, tile_cols), jnp.int32),
            pltpu.VMEM((tile_rows // 4, 128), F32),
            pltpu.VMEM((tile_rows // 4, 128), F32),
            pltpu.VMEM((tile_rows // 4 + 16, 128), F32),
            pltpu.VMEM((tile_rows // 4 + 16, 128), F32),
            pltpu.VMEM((num_cols,) + coarse, jnp.int32),
            pltpu.VMEM((group_layers, num_cols, cell_rows + 16, 128), F32),
            pltpu.VMEM((group_layers + 2, num_cols, cell_rows, 128), F32),
        ]
        + [slab] * 8
        + [
            pltpu.VMEM((2, num_cols) + coarse, F32),
            pltpu.VMEM((group_layers + 2, num_cols, cell_rows + 16, 128), F32),
            pltpu.VMEM((group_layers + 2, num_cols, cell_rows + 16, 128), F32),
            pltpu.VMEM((tile_cols, 128), BF16),
            pltpu.VMEM((8, 128, 128), BF16),
            pltpu.VMEM((cell_rows, tile_cols), F32),
            pltpu.VMEM((7, 2, num_cols, group_layers, 128), F32),
            pltpu.VMEM((7, 2, num_cols, group_layers, 128), F32),
            pltpu.VMEM((7, 2, 2, num_cols // 2, 8, 128), F32),
            pltpu.VMEM((7, 2, 2, num_cols // 2, 8, 128), F32),
            pltpu.VMEM((2,) + coarse, F32),
            pltpu.VMEM((2, num_cols) + coarse, F32),
            pltpu.VMEM((num_cols,) + coarse, F32),
            pltpu.VMEM((num_cols - 1,) + coarse, F32),
            pltpu.VMEM((3, cell_rows + 16, 128), F32),
            pltpu.VMEM((9, cell_rows + 16, 128), F32),
            pltpu.VMEM((9, cell_rows + 16, 128), F32),
            pltpu.SemaphoreType.DMA((11,)),
            pltpu.SemaphoreType.DMA((LINKS,)),
            pltpu.SemaphoreType.DMA((LINKS,)),
        ],
        compiler_params=pltpu.CompilerParams(
            collective_id=0, has_side_effects=True, vmem_limit_bytes=52 << 20
        ),
        name="coupled",
    )(demand, leakage, conductance, vias, layer_of, lateral_k, vertical_k)


def solution(mesh):
    in_specs = (
        P("row", "col"),
        P("row", "col"),
        P("row", "col"),
        P("row", "col"),
        P("row", None),
        P("col", "row", None),
        P("col", "row", None),
    )
    out_specs = (P("row", "col"), P("col", "row", None))
    step = functools.partial(body, mesh.shape["row"], mesh.shape["col"])
    return jax.shard_map(step, mesh=mesh, in_specs=in_specs, out_specs=out_specs, check_vma=False)
```

```python
import functools

import jax
import jax.numpy as jnp
from jax import lax
from jax.experimental import pallas as pl
from jax.experimental.pallas import tpu as pltpu
from jax.sharding import PartitionSpec as P

COARSE = 8
SWEEPS = 4
HEAT_SWEEPS = 4
COND_SLOPE = 0.5
LEAK_SLOPE = 0.7
VIA_CONDUCT = 4.0

MESH = pl.DeviceIdType.MESH
F32 = jnp.float32
BF16 = jnp.bfloat16
LINKS = 160
COEF_TILES = 4
HALVES = 2


def reciprocal(value):
    return 1.0 / value


def pooled(left, right):
    parts = []
    for _ in range(3):
        part = left.astype(BF16).astype(F32)
        parts.append(part)
        left = left - part
    count = left.shape[0]
    stacked = jnp.concatenate(parts, axis=0).astype(BF16)
    product = jnp.dot(stacked, right, preferred_element_type=F32)
    return (product[2 * count :] + product[count : 2 * count]) + product[:count]


def kernel(
    sizes,
    demand,
    leakage,
    conductance,
    vias,
    layer_of,
    lateral,
    vertical,
    drop_out,
    temp_out,
    p_cond,
    p_dem,
    p_leak,
    p_via,
    c_now,
    load,
    a_n,
    a_s,
    a_w,
    a_e,
    b_p,
    d_0,
    d_1,
    stage,
    stage_i,
    pl_send,
    pr_send,
    pl_recv,
    pr_recv,
    layers,
    lat,
    ver,
    t_n,
    t_s,
    t_w,
    t_e,
    t_b,
    t_a,
    t_r,
    b_t,
    r_far,
    temp_0,
    temp_1,
    pool,
    spread,
    rows_sum,
    rim_send,
    rim_recv,
    face_send,
    face_recv,
    heat_own,
    heat_all,
    part,
    part_recv,
    cell,
    g_up,
    e_up,
    load_sem,
    send_sem,
    recv_sem,
):
    NR, NC, TR, GL, CR = sizes
    NT = 8
    TQ = TR // 4
    row = lax.axis_index("row")
    col = lax.axis_index("col")
    up, down = lax.rem(row + NR - 1, NR), lax.rem(row + 1, NR)
    left, right = lax.rem(col + NC - 1, NC), lax.rem(col + 1, NC)
    peers = [lax.rem(col + k, NC) for k in range(1, NC)]
    count = [0]

    def send(src, dst, device):
        slot = count[0]
        count[0] += 1
        copy = pltpu.make_async_remote_copy(
            src_ref=src,
            dst_ref=dst,
            send_sem=send_sem.at[slot],
            recv_sem=recv_sem.at[slot],
            device_id=device,
            device_id_type=MESH,
        )
        copy.start()
        return copy

    lane = lax.broadcasted_iota(jnp.int32, (8, 128), 1)
    sub = lax.broadcasted_iota(jnp.int32, (8, 128), 0)
    first_lane = lane == 0
    last_lane = lane == 127

    def west_east(tiles):
        n = len(tiles)
        plus = [pltpu.roll(x, 1, axis=1) for x in tiles]
        minus = [pltpu.roll(x, 127, axis=1) for x in tiles]
        west = [jnp.where(first_lane, plus[t - 1], plus[t]) for t in range(n)]
        east = [jnp.where(last_lane, minus[(t + 1) % n], minus[t]) for t in range(n)]
        return west, east

    barrier = pltpu.get_barrier_semaphore()
    near = [(row, p) for p in peers]
    near += [(r, c) for r in (up, down) for c in (col, left, right)]
    for device in near:
        pl.semaphore_signal(barrier, inc=1, device_id=device, device_id_type=MESH)

    power = ((conductance, p_cond), (demand, p_dem), (leakage, p_leak), (vias, p_via))
    outer_tiles, inner_tiles = (0, NT - 1), tuple(range(1, NT - 1))

    def load_power(offset, tiles):
        for index, (src, dst) in enumerate(power):
            for t in tiles:
                pltpu.make_async_copy(
                    src.at[:, pl.ds(128 * t, 128)],
                    dst.at[t, pl.ds(16, TR), :],
                    load_sem.at[offset + index],
                ).start()
    load_power(0, outer_tiles)
    pl.semaphore_wait(barrier, len(near))

    row_copies = []
    for index, src in enumerate((conductance, demand, leakage, vias)):
        for side, start, device in ((0, TR - 8, (down, col)), (1, 0, (up, col))):
            dst = stage_i.at[side] if index == 3 else stage.at[side, index]
            row_copies.append(send(src.at[pl.ds(start, 8), :], dst, device))

    load_power(7, inner_tiles)
    for t in range(NC):
        cut = pl.ds(128 * t, 128)
        pltpu.make_async_copy(
            lateral.at[:, :, cut], lat.at[:, t, pl.ds(8, CR), :], load_sem.at[4]
        ).start()
        pltpu.make_async_copy(
            vertical.at[:, :, cut], ver.at[pl.ds(1, GL), t], load_sem.at[5]
        ).start()
        pltpu.make_async_copy(layer_of.at[:, cut], layers.at[t], load_sem.at[6]).start()

    def loaded(index, ref):
        pltpu.make_async_copy(ref, ref, load_sem.at[index]).wait()

    for index, (_, dst) in enumerate(power):
        loaded(index, dst.at[pl.ds(0, 2), pl.ds(16, TR), :])

    def pack_body(i, carry):
        base = pl.multiple_of(8 * i, 8)
        acc_l = acc_r = jnp.zeros((8, 128), F32)
        for q in range(4):
            for a, ref in enumerate((p_cond, p_dem, p_leak, p_via)):
                at = 32 * q + 8 * a
                rows = pl.ds(16 + q * TQ + base, 8)
                lo = ref[0, rows, :].astype(F32)
                hi = ref[NT - 1, rows, :].astype(F32)
                here = lane // 8 == at // 8
                acc_l = jnp.where(here, pltpu.roll(lo, at, axis=1), acc_l)
                acc_r = jnp.where(here, pltpu.roll(hi, (at + 8) % 128, axis=1), acc_r)
        pl_send[pl.ds(base, 8), :] = acc_l
        pr_send[pl.ds(base, 8), :] = acc_r
        return carry

    lax.fori_loop(0, TQ // 8, pack_body, 0)
    col_copies = []
    for src, dst, c in ((pl_send, pl_recv, left), (pr_send, pr_recv, right)):
        col_copies.append(send(src, dst.at[pl.ds(8, TQ), :], (row, c)))
        col_copies.append(send(src.at[pl.ds(TQ - 8, 8), :], dst.at[pl.ds(0, 8), :], (down, c)))
        col_copies.append(send(src.at[pl.ds(0, 8), :], dst.at[pl.ds(TQ + 8, 8), :], (up, c)))

    def send_rows(ref, first):
        span = pl.ds(first, GL)
        return [
            send(
                ref.at[span, :, pl.ds(8, 1), :], ref.at[span, :, pl.ds(8 + CR, 1), :], (up, col)
            ),
            send(
                ref.at[span, :, pl.ds(7 + CR, 1), :], ref.at[span, :, pl.ds(7, 1), :], (down, col)
            ),
        ]

    loaded(4, lat.at[:, :, pl.ds(8, CR), :])
    lat_copies = send_rows(lat, 0)
    ver_copies = []
    for t in range(NC):
        cut = pl.ds(128 * t, 128)
        ver_copies.append(send(vertical.at[GL - 1, :, cut], ver.at[0, t], (row, right)))
        ver_copies.append(send(vertical.at[0, :, cut], ver.at[GL + 1, t], (row, left)))

    def pool_body(i, carry):
        r = lax.broadcasted_iota(jnp.int32, (128, 128), 0)
        c = lax.broadcasted_iota(jnp.int32, (128, 128), 1)
        start = pl.multiple_of(i * 128, 128)
        pool[pl.ds(start, 128), :] = jnp.where(16 * i + r // 8 == c, 1.0 / 64.0, 0.0).astype(BF16)
        spread[i] = jnp.where(16 * i + c // 8 == r, 1.0, 0.0).astype(BF16)
        return carry

    lax.fori_loop(0, NT, pool_body, 0)
    for index, (_, dst) in enumerate(power):
        loaded(7 + index, dst.at[pl.ds(1, NT - 2), pl.ds(16, TR), :])

    for copy in row_copies + col_copies:
        copy.wait_recv()
    has_up = jnp.where(row > 0, 1.0, 0.0).astype(F32)
    has_down = jnp.where(row < NR - 1, 1.0, 0.0).astype(F32)
    side_ok = jnp.logical_or(
        jnp.logical_and(lane < 64, col < NC - 1), jnp.logical_and(lane >= 64, col > 0)
    )
    for index, ref in enumerate((p_cond, p_dem, p_leak)):
        for t in range(NT):
            cut = slice(128 * t, 128 * t + 128)
            top = stage[0, index, :, cut]
            bottom = stage[1, index, :, cut]
            if index == 0:
                top, bottom = top * has_up, bottom * has_down
            ref[t, 8:16, :] = top
            ref[t, 16 + TR : 24 + TR, :] = bottom
    for t in range(NT):
        cut = slice(128 * t, 128 * t + 128)
        p_via[t, 8:16, :] = stage_i[0, :, cut]
        p_via[t, 16 + TR : 24 + TR, :] = stage_i[1, :, cut]

    def rim(a, q, from_right, from_left):
        at = 32 * q + 8 * a
        value = jnp.where(
            lane < 64,
            pltpu.roll(from_right, (128 - at) % 128, axis=1),
            pltpu.roll(from_left, (248 - at) % 128, axis=1),
        )
        if a == 0:
            return jnp.where(side_ok, value, 0.0)
        if a == 3:
            return value.astype(jnp.int32)
        return value

    def unpack_body(i, carry):
        base = pl.multiple_of(8 * i, 8)
        from_right = pl_recv[pl.ds(8 + base, 8), :]
        from_left = pr_recv[pl.ds(8 + base, 8), :]
        for a, ref in enumerate((p_cond, p_dem, p_leak, p_via)):
            for q in range(4):
                ref[NT, pl.ds(16 + q * TQ + base, 8), :] = rim(a, q, from_right, from_left)
        return carry

    lax.fori_loop(0, TQ // 8, unpack_body, 0)
    for a, ref in enumerate((p_cond, p_dem, p_leak, p_via)):
        top = rim(a, 3, pl_recv[0:8, :], pr_recv[0:8, :])
        bottom = rim(a, 0, pl_recv[TQ + 8 : TQ + 16, :], pr_recv[TQ + 8 : TQ + 16, :])
        if a == 0:
            top, bottom = top * has_up, bottom * has_down
        ref[NT, 8:16, :] = top
        ref[NT, 16 + TR : 24 + TR, :] = bottom

    last_tile = TR // 8 + 1

    def power_coefs(c_ref, with_load):
        def coef_tile(i):
            base = pl.multiple_of(8 + 8 * i, 8)
            row_ok = jnp.logical_and(
                jnp.logical_or(i > 0, row > 0), jnp.logical_or(i < last_tile, row < NR - 1)
            )
            rows = pl.ds(base, 8)
            centers = [c_ref[t, rows, :] for t in range(NT + 1)]
            west, east = west_east(centers)
            for t in range(NT + 1):
                c = centers[t]
                c_n = c + c_ref[t, pl.ds(base - 1, 8), :]
                c_s = c + c_ref[t, pl.ds(base + 1, 8), :]
                c_w = c + west[t]
                c_e = c + east[t]
                denom = 0.5 * ((c_n + c_s) + (c_w + c_e)) + VIA_CONDUCT * p_via[
                    t, rows, :
                ].astype(F32)
                ok = row_ok if t < NT else jnp.logical_and(side_ok, row_ok)
                inverse = jnp.where(ok, reciprocal(denom), 0.0)
                half = 0.5 * inverse
                a_n[t, rows, :] = c_n * half
                a_s[t, rows, :] = c_s * half
                a_w[t, rows, :] = c_w * half
                a_e[t, rows, :] = c_e * half
                if with_load:
                    value = p_dem[t, rows, :] + p_leak[t, rows, :]
                    load[t, rows, :] = value
                else:
                    value = load[t, rows, :]
                b_p[t, rows, :] = value * inverse

        def coef_body(j, carry):
            for k in range(COEF_TILES):
                coef_tile(COEF_TILES * j + k)
            return carry

        lax.fori_loop(0, pl.cdiv(TR // 8 + 2, COEF_TILES), coef_body, 0)

    def power_sweep(src, dst):
        per = (TR // 8 + 2) // HALVES

        def sweep_body(j, carry):
            for i in range(per):
                base = pl.multiple_of(8 + 8 * (per * j + i), 8)
                rows = pl.ds(base, 8)
                west, east = west_east([src[t, rows, :] for t in range(NT + 1)])
                for t in range(NT + 1):
                    dst[t, rows, :] = (
                        b_p[t, rows, :]
                        + a_n[t, rows, :] * src[t, pl.ds(base - 1, 8), :]
                        + a_s[t, rows, :] * src[t, pl.ds(base + 1, 8), :]
                    ) + (a_w[t, rows, :] * west[t] + a_e[t, rows, :] * east[t])
            return carry

        lax.fori_loop(0, HALVES, sweep_body, 0)

    def send_heat(c_ref, d_ref, work, phase):
        def heat_body(i, carry):
            for k in range(4):
                rows = pl.ds(pl.multiple_of(16 + 32 * i + 8 * k, 8), 8)
                for t in range(NT):
                    d = d_ref[t, rows, :]
                    work[t, rows, :] = load[t, rows, :] * (1.0 - d) + c_ref[t, rows, :] * d * d
                    if phase == 1:
                        out_rows = pl.ds(pl.multiple_of(32 * i + 8 * k, 8), 8)
                        drop_out[out_rows, 128 * t : 128 * t + 128] = d
            return carry

        lax.fori_loop(0, TR // 32, heat_body, 0)
        for j in range(CR // 8):
            for t in range(NT):
                total = work[t, pl.ds(16 + 64 * j, 8, stride=8), :]
                for k in range(1, 8):
                    total = total + work[t, pl.ds(16 + 64 * j + k, 8, stride=8), :]
                rows_sum[8 * j : 8 * j + 8, 128 * t : 128 * t + 128] = total
        heat = pooled(rows_sum[...], pool[...])
        heat_own[phase] = heat
        heat_all[phase, col] = heat
        return [
            send(heat_own.at[phase], heat_all.at[phase, col], (row, peer)) for peer in peers
        ]

    def thermal_coefs(layer):
        low = jnp.logical_and(layer == 0, col == 0)
        high = jnp.logical_and(layer == GL - 1, col == NC - 1)
        for i in range(CR // 8):
            rows = pl.ds(8 * i, 8)
            centers = [lat[layer, t, pl.ds(8 + 8 * i, 8), :] for t in range(NC)]
            west, east = west_east(centers)
            for t in range(NC):
                k, k_w, k_e = centers[t], west[t], east[t]
                k_n = lat[layer, t, pl.ds(7 + 8 * i, 8), :]
                k_s = lat[layer, t, pl.ds(9 + 8 * i, 8), :]
                v = ver[layer + 1, t, rows, :]
                v_b = jnp.where(low, 0.0, ver[layer, t, rows, :])
                v_a = jnp.where(high, 0.0, ver[layer + 2, t, rows, :])
                edge_n = edge_s = edge_w = edge_e = None
                if i == 0:
                    edge_n = jnp.logical_and(sub == 0, row == 0)
                    k_n = jnp.where(edge_n, 0.0, k_n)
                if i == CR // 8 - 1:
                    edge_s = jnp.logical_and(sub == 7, row == NR - 1)
                    k_s = jnp.where(edge_s, 0.0, k_s)
                if t == 0:
                    edge_w = first_lane
                    k_w = jnp.where(edge_w, 0.0, k_w)
                if t == NC - 1:
                    edge_e = last_lane
                    k_e = jnp.where(edge_e, 0.0, k_e)
                sums = [k + k_n, k + k_s, k + k_w, k + k_e, v + v_b, v + v_a]
                twice = ((sums[0] + sums[1]) + (sums[2] + sums[3])) + (sums[4] + sums[5])
                inverse = reciprocal(twice)
                t_r[layer, t, rows, :] = 2.0 * inverse
                edges = (edge_n, edge_s, edge_w, edge_e, low, high)
                for ref, total, edge in zip((t_n, t_s, t_w, t_e, t_b, t_a), sums, edges):
                    value = total * inverse
                    if edge is not None:
                        value = jnp.where(edge, 0.0, value)
                    ref[layer, t, rows, :] = value

    def sources(phase, start):
        def source_body(layer, carry):
            for i in range(CR // 8):
                rows = pl.ds(8 * i, 8)
                for t in range(NC):
                    here = layers[t, rows, :] == col * GL + layer
                    value = (
                        jnp.where(here, heat_all[phase, t, rows, :], 0.0) * t_r[layer, t, rows, :]
                    )
                    b_t[layer, t, rows, :] = value
                    if start:
                        temp_0[layer + 1, t, pl.ds(8 + 8 * i, 8), :] = value
            return carry

        lax.fori_loop(0, GL, source_body, 0)
        if start:
            for side, target, layer in ((0, 0, -1), (1, GL + 1, GL)):
                for i in range(CR // 8):
                    rows = pl.ds(8 * i, 8)
                    for t in range(NC):
                        here = layers[t, rows, :] == col * GL + layer
                        temp_0[target, t, pl.ds(8 + 8 * i, 8), :] = (
                            jnp.where(here, heat_all[phase, t, rows, :], 0.0)
                            * r_far[side, t, rows, :]
                        )

    half = NC // 2
    chunks = (range(half), range(half, NC))
    tall = CR // 8
    edge_tiles = sorted({0, tall - 1})
    mid_tiles = [i for i in range(tall) if i not in edge_tiles]

    def thermal_block(src, dst, first, depth, row_tiles, tiles, out=None):
        cache = {}

        def at(k, i, t):
            if (k, i, t) not in cache:
                cache[k, i, t] = src[first + k, t, pl.ds(8 + 8 * i, 8), :]
            return cache[k, i, t]

        for k in range(depth):
            layer = first + k
            for i in row_tiles:
                rows = pl.ds(8 * i, 8)
                plus = {
                    t: pltpu.roll(at(k + 1, i, t), 1, axis=1)
                    for t in range(max(tiles[0] - 1, 0), tiles[-1] + 1)
                }
                minus = {
                    t: pltpu.roll(at(k + 1, i, t), 127, axis=1)
                    for t in range(tiles[0], min(tiles[-1] + 2, NC))
                }
                for t in tiles:
                    west = plus[t] if t == 0 else jnp.where(first_lane, plus[t - 1], plus[t])
                    east = minus[t] if t == NC - 1 else jnp.where(last_lane, minus[t + 1], minus[t])
                    value = (
                        (
                            b_t[layer, t, rows, :]
                            + t_n[layer, t, rows, :] * src[layer + 1, t, pl.ds(7 + 8 * i, 8), :]
                        )
                        + (
                            t_s[layer, t, rows, :] * src[layer + 1, t, pl.ds(9 + 8 * i, 8), :]
                            + t_b[layer, t, rows, :] * at(k, i, t)
                        )
                        + (t_a[layer, t, rows, :] * at(k + 2, i, t))
                        + (t_w[layer, t, rows, :] * west + t_e[layer, t, rows, :] * east)
                    )
                    if out is None:
                        dst[layer + 1, t, pl.ds(8 + 8 * i, 8), :] = value
                    else:
                        out[layer, rows, 128 * t : 128 * t + 128] = value

    def inner_layers(src, dst, row_tiles, out=None):
        depth = (GL - 2) // 2

        def inner_body(j, carry):
            thermal_block(src, dst, 1 + depth * j, depth, row_tiles, range(NC), out)
            return carry

        if row_tiles:
            lax.fori_loop(0, 2, inner_body, 0)

    def send_planes(ref, chunk):
        mid, tiles = pl.ds(8, CR), pl.ds(chunk[0], len(chunk))
        return [
            send(ref.at[GL, tiles, mid, :], ref.at[0, tiles, mid, :], (row, right)),
            send(ref.at[1, tiles, mid, :], ref.at[GL + 1, tiles, mid, :], (row, left)),
        ]

    def copy_rims(ref, level, layer_list, tiles, buffer, place, put):
        for layer, slot in layer_list:
            for t in tiles:
                for side, inside, outside in ((0, 8, 8 + CR), (1, 7 + CR, 7)):
                    if put:
                        ref[layer + 1, t, pl.ds(outside, 1), :] = buffer[place(side, t, slot)]
                    else:
                        buffer[place(side, t, slot)] = ref[layer + 1, t, pl.ds(inside, 1), :]

    def inner_rims(ref, level, buffer, put):
        def rim_body(layer, carry):
            copy_rims(
                ref,
                level,
                ((layer, layer),),
                range(NC),
                buffer,
                lambda side, t, slot: (level - 1, side, t, pl.ds(slot, 1), slice(None)),
                put,
            )
            return carry

        lax.fori_loop(1, GL - 1, rim_body, 0)

    def face_rims(ref, level, index, buffer, put):
        copy_rims(
            ref,
            level,
            ((0, 0), (GL - 1, 1)),
            chunks[index],
            buffer,
            lambda side, t, slot: (
                level - 1,
                side,
                index,
                t - chunks[index][0],
                pl.ds(slot, 1),
                slice(None),
            ),
            put,
        )

    def send_inner(ref, level):
        inner_rims(ref, level, rim_send, False)
        return [
            send(rim_send.at[level - 1, side], rim_recv.at[level - 1, side], (r, col))
            for side, r in ((0, up), (1, down))
        ]

    def send_face(ref, level, index):
        face_rims(ref, level, index, face_send, False)
        cut = pl.ds(0, 2)
        return [
            send(
                face_send.at[level - 1, side, index, :, cut, :],
                face_recv.at[level - 1, side, index, :, cut, :],
                (r, col),
            )
            for side, r in ((0, up), (1, down))
        ]

    def faces(body):
        def face_body(j, carry):
            body(j * (GL - 1))
            return carry

        lax.fori_loop(0, 2, face_body, 0)

    def interior(body):
        def interior_body(j, carry):
            body(j)
            return carry

        lax.fori_loop(1, GL - 1, interior_body, 0)

    power_coefs(p_cond, True)
    loaded(5, ver.at[pl.ds(1, GL)])
    loaded(6, layers)
    for copy in ver_copies + lat_copies:
        copy.wait_recv()
    faces(thermal_coefs)
    r_copies = [
        send(t_r.at[GL - 1], r_far.at[0], (row, right)),
        send(t_r.at[0], r_far.at[1], (row, left)),
    ]
    power_sweep(b_p, d_0)
    power_sweep(d_0, d_1)
    power_sweep(d_1, d_0)
    heat_copies = send_heat(p_cond, d_0, d_1, 0)
    interior(thermal_coefs)
    for copy in heat_copies + r_copies:
        copy.wait_recv()
    sources(0, True)
    pending = list(row_copies + col_copies + ver_copies + lat_copies + r_copies + heat_copies)

    face_copies = {1: [send_face(temp_0, 1, index) for index in range(2)]}
    rims = {1: send_inner(temp_0, 1)}
    planes = {}

    def sweep(level, exchange=True, out=None):
        src, dst = (temp_0, temp_1) if level % 2 == 0 else (temp_1, temp_0)
        for copies in planes.get(level - 2, ()):
            for copy in copies:
                copy.wait_send()
        planes_now, faces_now = [], []
        for index, chunk in enumerate(chunks):
            for copy in face_copies[level - 1][index]:
                copy.wait_recv()
            if level - 1 in planes:
                for copy in planes[level - 1][index]:
                    copy.wait_recv()
            face_rims(src, level - 1, index, face_recv, True)
            for layer in (0, GL - 1):
                thermal_block(src, dst, layer, 1, range(tall), chunk, out)
            if exchange:
                planes_now.append(send_planes(dst, chunk))
                faces_now.append(send_face(dst, level, index))
        for copy in rims[level - 1]:
            copy.wait_recv()
        inner_rims(src, level - 1, rim_recv, True)
        if exchange:
            planes[level], face_copies[level] = planes_now, faces_now
            inner_layers(src, dst, edge_tiles)
            rims[level] = send_inner(dst, level)
            inner_layers(src, dst, mid_tiles)
        else:
            inner_layers(src, dst, list(range(tall)), out)

    sweep(2)
    sweep(3)
    sweep(4, False)

    def part_body(i, carry):
        base = pl.multiple_of(8 * i, 8)
        for t in range(NC):
            ids = layers[t, pl.ds(base, 8), :] - col * GL
            total = jnp.zeros((8, 128), F32)
            for layer in range(GL):
                total = jnp.where(
                    ids == layer, temp_1[layer + 1, t, pl.ds(8 + base, 8), :], total
                )
            part[t, pl.ds(base, 8), :] = total
        return carry

    lax.fori_loop(0, CR // 8, part_body, 0)
    part_copies = [
        send(part.at[peer], part_recv.at[k], (row, peer)) for k, peer in enumerate(peers)
    ]
    for copy in part_copies:
        copy.wait_recv()
    total = part[col]
    for k in range(NC - 1):
        total = total + part_recv[k]
    cell[1, 8 : 8 + CR, :] = total
    own = cell.at[1, pl.ds(8, CR), :]
    low_rows = cell.at[1, pl.ds(8, 8), :]
    high_rows = cell.at[1, pl.ds(CR, 8), :]
    above, below = pl.ds(0, 8), pl.ds(8 + CR, 8)
    cell_copies = [
        send(own, cell.at[0, pl.ds(8, CR), :], (row, right)),
        send(own, cell.at[2, pl.ds(8, CR), :], (row, left)),
    ]
    for place, c in ((1, col), (0, right), (2, left)):
        cell_copies.append(send(high_rows, cell.at[place, above, :], (down, c)))
        cell_copies.append(send(low_rows, cell.at[place, below, :], (up, c)))
    shapes = (
        (g_up, lambda x: reciprocal(1.0 + COND_SLOPE * x)),
        (e_up, lambda x: jnp.exp(LEAK_SLOPE * x)),
    )
    for target, shape in shapes:
        coarse = shape(total)
        for t in range(NT):
            target[t, 8 : 8 + CR, :] = pooled(coarse, spread[t])

    def warm_tile(i, tiles):
        rows = pl.ds(pl.multiple_of(8 + 8 * i, 8), 8)
        coarse = pl.ds(7 + i, 1)
        for t in tiles:
            c_now[t, rows, :] = p_cond[t, rows, :] * g_up[t, coarse, :]
            load[t, rows, :] = p_dem[t, rows, :] + p_leak[t, rows, :] * e_up[t, coarse, :]

    def warm_body(j, carry):
        for k in range(4):
            warm_tile(1 + 4 * j + k, range(NT))
        return carry

    lax.fori_loop(0, TR // 32, warm_body, 0)
    for copy in cell_copies:
        copy.wait_recv()
    for target, shape in shapes:
        coarse = shape(jnp.concatenate([cell[1, 0:8, :], cell[1, 8 + CR : 16 + CR, :]], axis=0))
        for t in range(NT):
            rims_up = pooled(coarse, spread[t])
            target[t, 0:8, :] = rims_up[0:8]
            target[t, 8 + CR : 16 + CR, :] = rims_up[8:16]
        from_left = jnp.broadcast_to(shape(cell[0])[:, 127:128], (CR + 16, 128))
        from_right = jnp.broadcast_to(shape(cell[2])[:, 0:1], (CR + 16, 128))
        wide = lax.broadcasted_iota(jnp.int32, (CR + 16, 128), 1)
        target[NT] = jnp.where(wide < 64, from_right, from_left)
    warm_tile(0, range(NT))
    warm_tile(last_tile, range(NT))

    def warm_side_body(j, carry):
        for k in range(2):
            warm_tile(2 * j + k, (NT,))
        return carry

    lax.fori_loop(0, TR // 16 + 1, warm_side_body, 0)

    planes[4] = [send_planes(temp_1, chunk) for chunk in chunks]
    face_copies[4] = [send_face(temp_1, 4, index) for index in range(2)]
    rims[4] = send_inner(temp_1, 4)
    power_coefs(c_now, False)
    power_sweep(d_0, d_1)
    power_sweep(d_1, d_0)
    power_sweep(d_0, d_1)
    power_sweep(d_1, d_0)
    heat_copies = send_heat(c_now, d_0, d_1, 1)
    for copy in heat_copies:
        copy.wait_recv()
    sources(1, False)
    pending += part_copies + cell_copies + heat_copies
    sweep(5)
    sweep(6)
    sweep(7)
    sweep(8, False, temp_out)
    for copies in rims.values():
        pending += copies
    for pair in face_copies.values():
        for copies in pair:
            pending += copies
    for copies in planes[7]:
        pending += copies
    for copy in pending:
        copy.wait_send()


def body(num_rows, num_cols, demand, leakage, conductance, vias, layer_of, lateral_k, vertical_k):
    tile_rows, tile_cols = demand.shape
    group_layers, cell_rows, therm_cols = lateral_k.shape
    sizes = (num_rows, num_cols, tile_rows, group_layers, cell_rows)
    fine = pltpu.VMEM((9, tile_rows + 48, 128), F32)
    slab = pltpu.VMEM((group_layers, num_cols, cell_rows, 128), F32)
    coarse = (cell_rows, 128)
    hbm = pl.BlockSpec(memory_space=pl.ANY)
    return pl.pallas_call(
        functools.partial(kernel, sizes),
        out_shape=(
            jax.ShapeDtypeStruct(demand.shape, F32),
            jax.ShapeDtypeStruct(lateral_k.shape, F32),
        ),
        in_specs=[hbm] * 7,
        out_specs=(pl.BlockSpec(memory_space=pltpu.VMEM),) * 2,
        scratch_shapes=[fine] * 3
        + [pltpu.VMEM((9, tile_rows + 48, 128), jnp.int32)]
        + [fine] * 9
        + [
            pltpu.VMEM((2, 3, 8, tile_cols), F32),
            pltpu.VMEM((2, 8, tile_cols), jnp.int32),
            pltpu.VMEM((tile_rows // 4, 128), F32),
            pltpu.VMEM((tile_rows // 4, 128), F32),
            pltpu.VMEM((tile_rows // 4 + 16, 128), F32),
            pltpu.VMEM((tile_rows // 4 + 16, 128), F32),
            pltpu.VMEM((num_cols,) + coarse, jnp.int32),
            pltpu.VMEM((group_layers, num_cols, cell_rows + 16, 128), F32),
            pltpu.VMEM((group_layers + 2, num_cols, cell_rows, 128), F32),
        ]
        + [slab] * 8
        + [
            pltpu.VMEM((2, num_cols) + coarse, F32),
            pltpu.VMEM((group_layers + 2, num_cols, cell_rows + 16, 128), F32),
            pltpu.VMEM((group_layers + 2, num_cols, cell_rows + 16, 128), F32),
            pltpu.VMEM((tile_cols, 128), BF16),
            pltpu.VMEM((8, 128, 128), BF16),
            pltpu.VMEM((cell_rows, tile_cols), F32),
            pltpu.VMEM((7, 2, num_cols, group_layers, 128), F32),
            pltpu.VMEM((7, 2, num_cols, group_layers, 128), F32),
            pltpu.VMEM((7, 2, 2, num_cols // 2, 8, 128), F32),
            pltpu.VMEM((7, 2, 2, num_cols // 2, 8, 128), F32),
            pltpu.VMEM((2,) + coarse, F32),
            pltpu.VMEM((2, num_cols) + coarse, F32),
            pltpu.VMEM((num_cols,) + coarse, F32),
            pltpu.VMEM((num_cols - 1,) + coarse, F32),
            pltpu.VMEM((3, cell_rows + 16, 128), F32),
            pltpu.VMEM((9, cell_rows + 16, 128), F32),
            pltpu.VMEM((9, cell_rows + 16, 128), F32),
            pltpu.SemaphoreType.DMA((11,)),
            pltpu.SemaphoreType.DMA((LINKS,)),
            pltpu.SemaphoreType.DMA((LINKS,)),
        ],
        compiler_params=pltpu.CompilerParams(
            collective_id=0, has_side_effects=True, vmem_limit_bytes=52 << 20
        ),
        name="coupled",
    )(demand, leakage, conductance, vias, layer_of, lateral_k, vertical_k)


def solution(mesh):
    in_specs = (
        P("row", "col"),
        P("row", "col"),
        P("row", "col"),
        P("row", "col"),
        P("row", None),
        P("col", "row", None),
        P("col", "row", None),
    )
    out_specs = (P("row", "col"), P("col", "row", None))
    step = functools.partial(body, mesh.shape["row"], mesh.shape["col"])
    return jax.shard_map(step, mesh=mesh, in_specs=in_specs, out_specs=out_specs, check_vma=False)
```
